128 devices in a mesh: row: 8 (over x, core), col: 16 (over y, z).
Axes of the slice: x: 4, y: 4, z: 4, core: 2. Of those that a mesh axis runs over, the one named last changes fastest.
Arguments:
- root_inverse: float32 [4096, 4096], P('row', 'col'), as said below
- factor_one: float32 [16, 1024, 192], P('row'), may hold values from -0.1875 to 0.1875
- pivot_one: float32 [16, 192, 192], P('row'), as said below
- pattern_one: int32 [16, 16], P('row'), may hold values from 0 to 63, as said below
- factor_two: float32 [16, 16, 384, 192], P('row', 'col'), may hold values from -0.3125 to 0.3125
- pivot_two: float32 [16, 16, 192, 192], P('row', 'col'), as said below
- pattern_two: int32 [16, 16, 6], P('row'), may hold values from 0 to 18, as said below
Outputs:
- column_one: float32 [16, 1024, 192], P('row')
- diagonal_one: float32 [16, 192, 192], P('row')
- column_two: float32 [16, 16, 384, 192], P('row', 'col')
- diagonal_two: float32 [16, 16, 192, 192], P('row', 'col')
The draws below stay inside these ranges and needn't reach their ends.
Inputs may be any that keep to these rules, and one draw needn't show every extreme that they name: `root_inverse`: symmetric. `pivot_one`: symmetric. `pivot_two`: symmetric. `pattern_one`: each row holds 16 different blocks in increasing order. `pattern_two`: each row holds 6 different blocks in increasing order.
All inputs are finite; a program needn't handle non-finite values.
Results may differ from the reference program's by a relative error of at most 0.0003.
Values sent between devices are 32-bit elements; how exact they have to be, the bound alone decides.
No kernel may reach another device: no remote copies, remote signals or barrier semaphores. Data moves between devices by JAX's collectives and lax.ppermute only.
A program may use at most 128 MiB of HBM per device.

```python
import math
import jax
import jax.numpy as jnp
from jax import lax

BLOCK_ROWS = 64
SUPER_WIDTH = 192
BLOCKS_ONE = 16
BLOCKS_TWO = 6
ROOT_BLOCKS = 64
PARENTS = 16
CHILDREN = 16
ROOT_ROWS = 4096
EXT_BLOCKS = 19


def symmetric(key, leading, order):
    first = jax.random.fold_in(key, 0)
    third = jax.random.fold_in(key, 2)
    normal_part = jax.random.normal(first, leading + (order, order), jnp.float32)
    mixture = normal_part
    mixture = (mixture + jnp.swapaxes(mixture, -1, -2)) * (0.3 / math.sqrt(order))
    diagonal = jax.random.uniform(third, leading + (order,), jnp.float32, 1.0, 2.0)
    identity = jnp.eye(order, dtype=jnp.float32)
    return mixture + identity * diagonal[..., None]


def draw_root_inverse(key, part):
    key = jax.random.fold_in(key, 3)
    return symmetric(key, (), ROOT_ROWS)


def draw_pivot_one(key, part):
    key = jax.random.fold_in(key, 5)
    return symmetric(key, (PARENTS,), SUPER_WIDTH)


def draw_pivot_two(key, part):
    key = jax.random.fold_in(key, 7)
    return symmetric(key, (PARENTS, CHILDREN), SUPER_WIDTH)


def draw_pattern_one(key, part):
    key = jax.random.fold_in(key, 11)
    keys = jax.random.split(key, PARENTS)
    orders = jax.vmap(lambda single: jax.random.permutation(single, ROOT_BLOCKS))(keys)
    return jnp.sort(orders[:, :BLOCKS_ONE], axis=1).astype(jnp.int32)


def draw_pattern_two(key, part):
    key = jax.random.fold_in(key, 13)
    keys = jax.random.split(key, PARENTS * CHILDREN)
    orders = jax.vmap(lambda single: jax.random.permutation(single, EXT_BLOCKS))(keys)
    picked = jnp.sort(orders[:, :BLOCKS_TWO], axis=1).astype(jnp.int32)
    return picked.reshape(PARENTS, CHILDREN, BLOCKS_TWO)


def block_scale(key, shape, pieces, low, largest):
    gain, own = 1.0, jax.random.fold_in(key, 6)
    for axis_at, blocks in pieces:
        heights = jnp.exp(jax.random.uniform(jax.random.fold_in(own, axis_at), (blocks,), jnp.float32, low / len(pieces), largest / len(pieces)))
        gain = gain * jnp.repeat(heights, shape[axis_at] // blocks).reshape([-1 if axis == axis_at else 1 for axis in range(len(shape))])
    return gain


def gaussian(own_key, shape, width, reach, cuts=(), kind=jnp.bfloat16):
    gain = block_scale(own_key, shape, cuts, -0.22, 0.18) if cuts else 1.0
    result = jax.random.normal(own_key, shape, jnp.float32) * width * gain
    return jnp.minimum(jnp.maximum(result, -reach), reach).astype(kind)


def setup_inputs(seed: int = 0) -> dict:
    key_list = jax.random.split(jax.random.key(seed), 8)
    return {
        "root_inverse": draw_root_inverse(jax.random.fold_in(key_list[7], 71), 0),
        "factor_one": gaussian(key_list[1], (PARENTS, BLOCKS_ONE * BLOCK_ROWS, SUPER_WIDTH), (BLOCKS_ONE * BLOCK_ROWS) ** -0.5, 0.1875, ((0, 8),), jnp.float32),
        "pivot_one": draw_pivot_one(jax.random.fold_in(key_list[7], 71), 0),
        "pattern_one": draw_pattern_one(jax.random.fold_in(key_list[7], 71), 0),
        "factor_two": gaussian(key_list[4], (PARENTS, CHILDREN, BLOCKS_TWO * BLOCK_ROWS, SUPER_WIDTH), (BLOCKS_TWO * BLOCK_ROWS) ** -0.5, 0.3125, ((0, 8), (1, 16)), jnp.float32),
        "pivot_two": draw_pivot_two(jax.random.fold_in(key_list[7], 71), 0),
        "pattern_two": draw_pattern_two(jax.random.fold_in(key_list[7], 71), 0),
    }


def block_rows(blocks, size):
    offsets = jnp.arange(size, dtype=jnp.int32)
    return (blocks.astype(jnp.int32)[:, None] * size + offsets[None, :]).reshape(-1)


def reference(root_inverse, factor_one, pivot_one, pattern_one, factor_two, pivot_two, pattern_two):
    precise = lax.Precision.HIGHEST

    def parent_step(inputs):
        factor, pivot_block, pattern, child_factors, child_pivots, child_patterns = inputs
        row_ids = block_rows(pattern, BLOCK_ROWS)
        interior = jnp.take(jnp.take(root_inverse, row_ids, axis=0), row_ids, axis=1)
        column = -jnp.dot(interior, factor, precision=precise, preferred_element_type=jnp.float32)
        diagonal = pivot_block - jnp.dot(factor.T, column, precision=precise, preferred_element_type=jnp.float32)
        upper_rows = jnp.concatenate([diagonal, column.T], axis=1)
        lower_rows = jnp.concatenate([column, interior], axis=1)
        extended = jnp.concatenate([upper_rows, lower_rows], axis=0)

        def child_step(child_inputs):
            child_factor, child_pivot, child_pattern = child_inputs
            child_rows = block_rows(child_pattern, BLOCK_ROWS)
            selected = jnp.take(jnp.take(extended, child_rows, axis=0), child_rows, axis=1)
            child_column = -jnp.dot(selected, child_factor, precision=precise, preferred_element_type=jnp.float32)
            child_diagonal = child_pivot - jnp.dot(child_factor.T, child_column, precision=precise, preferred_element_type=jnp.float32)
            return child_column, child_diagonal

        child_columns, child_diagonals = lax.map(child_step, (child_factors, child_pivots, child_patterns))
        return column, diagonal, child_columns, child_diagonals

    column_one, diagonal_one, column_two, diagonal_two = lax.map(
        parent_step, (factor_one, pivot_one, pattern_one, factor_two, pivot_two, pattern_two))
    return (column_one, diagonal_one, column_two, diagonal_two)
```

```python
import jax
import jax.numpy as jnp
from jax import lax
from jax.experimental import pallas as pl
from jax.experimental.pallas import tpu as pltpu
from jax.sharding import PartitionSpec as P

F32 = jnp.float32
BF16 = jnp.bfloat16
BLOCK = 64
WIDTH = 192
ONE = 16
TWO = 6
OWN = 3
COLS = 16
ROWS = 8
SLICE = 4
CHILD_ROWS = 2 * TWO * SLICE
BAND = ONE * SLICE
MESSAGE = CHILD_ROWS + BAND
WIDE = TWO * BLOCK
VMEM = pl.BlockSpec(memory_space=pltpu.VMEM)
SMEM = pl.BlockSpec(memory_space=pltpu.SMEM)
ANY = pl.BlockSpec(memory_space=pl.ANY)


def split(value):
    high = value.astype(BF16)
    low = (value - high.astype(F32)).astype(BF16)
    return high, low


def product(left, right, dims=((1,), (0,))):
    def one(a, b):
        return lax.dot_general(a, b, (dims, ((), ())), preferred_element_type=F32)

    (lh, ll), (rh, rl) = left, right
    return one(lh, rh) + (one(lh, rl) + one(ll, rh))


def pack_kernel(root_ref, first_ref, second_ref):
    for place in range(COLS):
        for n in range(4):
            first_ref[place, n] = root_ref[pl.ds(BLOCK * n + place, SLICE, stride=16), :]
            second_ref[place, n] = root_ref[pl.ds(256 + BLOCK * n + place, SLICE, stride=16), :]


def pack(root):
    shape = jax.ShapeDtypeStruct((COLS, 4, SLICE, 256), F32)
    return pl.pallas_call(
        pack_kernel,
        grid=(2,),
        out_shape=(shape, shape),
        in_specs=[pl.BlockSpec((512, 128), lambda tile: (0, tile))],
        out_specs=(pl.BlockSpec((COLS, 4, SLICE, 128), lambda tile: (0, 0, 0, tile)),) * 2,
        name="pack",
    )(root)


def select_kernel(slots_ref, one_ref, two_ref, factor_ref, *refs):
    pieces, (out_ref, raw, band, sems) = refs[:16], refs[16:]
    copies = [
        pltpu.make_async_copy(piece, raw.at[slots_ref[n]], sems.at[n])
        for n, piece in enumerate(pieces)
    ]
    for copy in copies:
        copy.start()
    for copy in copies:
        copy.wait()
    left_half = lax.broadcasted_iota(jnp.int32, (SLICE, 128), 1) < BLOCK
    for parent in range(2):
        for a in range(ONE):
            row_block = one_ref[parent, a]
            slot = row_block // 4
            row = row_block % 4
            for pair in range(ONE // 2):
                halves = []
                for side in range(2):
                    block = one_ref[parent, 2 * pair + side]
                    tile = pl.multiple_of(128 * ((block % 4) // 2), 128)
                    value = raw[slot, block // 4, row, :, pl.ds(tile, 128)]
                    turn = BLOCK * ((block + side) % 2)
                    halves.append(pltpu.roll(value, turn, 1))
                band[0, parent, a, :, pair * 128 : pair * 128 + 128] = jnp.where(
                    left_half, halves[0], halves[1]
                )
    for parent in range(2):
        for pair in range(ONE // 2):
            lanes = slice(pair * 128, pair * 128 + 128)
            band[1, parent, :, :, lanes] = pltpu.roll(band[0, parent, :, :, lanes], BLOCK, 2)
    columns = jnp.concatenate(
        [
            -product(
                split(band[0, parent].reshape(BAND, ONE * BLOCK)), split(factor_ref[parent])
            )
            for parent in range(2)
        ],
        axis=1,
    )
    for child in range(COLS):
        for tile in range(3):
            top = tile * MESSAGE + CHILD_ROWS
            out_ref[child, top : top + BAND, :] = columns[:, 128 * tile : 128 * tile + 128]

    def child_step(child, carry):
        for parent in range(2):
            picks = [
                jnp.maximum(two_ref[parent, child, n] - OWN, 0) for n in range(TWO)
            ]
            for k in range(TWO):
                for pair in range(TWO // 2):
                    halves = []
                    for side in range(2):
                        block = picks[2 * pair + side]
                        tile = pl.multiple_of(128 * (block // 2), 128)
                        turned = (block + side) % 2
                        halves.append(band[turned, parent, picks[k], :, pl.ds(tile, 128)])
                    top = pair * MESSAGE + (parent * TWO + k) * SLICE
                    out_ref[child, top : top + SLICE, :] = jnp.where(
                        left_half, halves[0], halves[1]
                    )
        return carry

    lax.fori_loop(0, COLS, child_step, 0)


def select(slots, pattern_one, pattern_two, factor, pieces):
    return pl.pallas_call(
        select_kernel,
        out_shape=jax.ShapeDtypeStruct((COLS, 3 * MESSAGE, 128), F32),
        in_specs=[SMEM, SMEM, SMEM, VMEM] + [ANY] * 16,
        out_specs=VMEM,
        scratch_shapes=[
            pltpu.VMEM((16, COLS, 4, SLICE, 256), F32),
            pltpu.VMEM((2, 2, ONE, SLICE, ONE * BLOCK), F32),
            pltpu.SemaphoreType.DMA((16,)),
        ],
        compiler_params=pltpu.CompilerParams(vmem_limit_bytes=40 * 2**20),
        name="select",
    )(slots, pattern_one, pattern_two, factor, *pieces)


def final_kernel(
    two_ref, got_ref, factor_ref, pivot_ref, child_factor_ref, child_pivot_ref,
    column_ref, diagonal_ref, child_column_ref, child_diagonal_ref, chosen, mixed,
):
    left_half = lax.broadcasted_iota(jnp.int32, (16, 128), 1) < BLOCK
    for n in range(BAND):
        tiles = [
            got_ref[pl.ds(m * MESSAGE + CHILD_ROWS + n, 16, stride=3 * MESSAGE), :]
            for m in range(3)
        ]
        here = slice(16 * n, 16 * n + 16)
        column_ref[0, here, 0:128] = tiles[0]
        column_ref[0, here, 128:192] = tiles[1][:, :64]
        turned = [pltpu.roll(tile, BLOCK, 1) for tile in tiles[1:]]
        column_ref[1, here, 0:128] = jnp.where(left_half, turned[0], turned[1])
        column_ref[1, here, 128:192] = turned[1][:, :64]
    for parent in range(2):
        diagonal_ref[parent] = pivot_ref[parent] - product(
            split(factor_ref[parent]), split(column_ref[parent]), ((0,), (0,))
        )
        for n in range(TWO * SLICE):
            for m in range(3):
                start = m * MESSAGE + parent * TWO * SLICE + n
                chosen[16 * n : 16 * n + 16, 128 * m : 128 * m + 128] = got_ref[
                    pl.ds(start, 16, stride=3 * MESSAGE), :
                ]
        picks = [two_ref[parent, n] for n in range(TWO)]
        factors = [child_factor_ref[parent, 0, BLOCK * n : BLOCK * n + BLOCK, :] for n in range(TWO)]
        outside = jnp.concatenate(
            [jnp.where(picks[n] >= OWN, factors[n], 0.0) for n in range(TWO)], axis=0
        )
        inside = jnp.concatenate(
            [
                sum(jnp.where(picks[n] == e, factors[n], 0.0) for n in range(TWO))
                for e in range(OWN)
            ],
            axis=0,
        )
        below = jnp.concatenate(
            [
                column_ref[
                    parent,
                    pl.ds(pl.multiple_of(BLOCK * jnp.maximum(picks[n] - OWN, 0), BLOCK), BLOCK),
                    :,
                ]
                for n in range(TWO)
            ],
            axis=0,
        )
        outside, inside, below = split(outside), split(inside), split(below)
        lower = product(split(chosen[...]), outside) + product(below, inside)
        mixed[...] = product(split(diagonal_ref[parent]), inside) + product(
            below, outside, ((0,), (0,))
        )
        for n in range(TWO):
            own = mixed[
                pl.ds(pl.multiple_of(BLOCK * jnp.minimum(picks[n], OWN - 1), BLOCK), BLOCK), :
            ]
            child_column_ref[parent, 0, BLOCK * n : BLOCK * n + BLOCK, :] = -jnp.where(
                picks[n] >= OWN, lower[BLOCK * n : BLOCK * n + BLOCK], own
            )
        child_diagonal_ref[parent, 0] = child_pivot_ref[parent, 0] - product(
            split(child_factor_ref[parent, 0]), split(child_column_ref[parent, 0]), ((0,), (0,))
        )


def finish(own_two, got, factor, pivot, child_factor, child_pivot):
    return pl.pallas_call(
        final_kernel,
        out_shape=(
            jax.ShapeDtypeStruct((2, ONE * BLOCK, WIDTH), F32),
            jax.ShapeDtypeStruct((2, WIDTH, WIDTH), F32),
            jax.ShapeDtypeStruct((2, 1, WIDE, WIDTH), F32),
            jax.ShapeDtypeStruct((2, 1, WIDTH, WIDTH), F32),
        ),
        in_specs=[SMEM] + [VMEM] * 5,
        out_specs=(VMEM,) * 4,
        scratch_shapes=[pltpu.VMEM((WIDE, WIDE), F32), pltpu.VMEM((WIDTH, WIDTH), F32)],
        compiler_params=pltpu.CompilerParams(vmem_limit_bytes=40 * 2**20),
        name="finish",
    )(own_two, got, factor, pivot, child_factor, child_pivot)


FORWARD = [(r, (r + 2) % ROWS) for r in range(ROWS)]
BACKWARD = [(r, (r - 2) % ROWS) for r in range(ROWS)]
SWAP = [(r, r ^ 1) for r in range(ROWS)]


def per_device(
    root_inverse, factor_one, pivot_one, pattern_one, factor_two, pivot_two, pattern_two
):
    row = lax.axis_index("row")
    col = lax.axis_index("col")
    shards = [
        lax.all_to_all(part, "col", 0, 0, tiled=True)
        for part in pack(root_inverse)
    ]
    ahead = [lax.ppermute(part, "row", FORWARD) for part in shards]
    behind = [lax.ppermute(part, "row", BACKWARD) for part in shards]
    across = [lax.ppermute(ahead[0], "row", FORWARD), lax.ppermute(behind[1], "row", BACKWARD)]
    pieces, places = [], []
    for near, shift in ((shards, 0), (ahead, -2), (behind, 2), (across, 4)):
        for half in range(2):
            place = (row + shift) % ROWS
            pieces += [near[half], lax.ppermute(near[half], "row", SWAP)]
            places += [2 * place + half, 2 * (place ^ 1) + half]
    slots = jnp.stack(places).astype(jnp.int32)
    message = select(slots, pattern_one, pattern_two, factor_one, pieces)
    got = lax.all_to_all(message, "col", 0, 0, tiled=True)
    own_two = lax.dynamic_index_in_dim(pattern_two, col, 1, keepdims=False)
    return finish(
        own_two, got.reshape(COLS * 3 * MESSAGE, 128), factor_one, pivot_one, factor_two, pivot_two
    )


def solution(mesh):
    placed = (
        P("row", "col"),
        P("row", None, None),
        P("row", None, None),
        P("row", None),
        P("row", "col", None, None),
        P("row", "col", None, None),
        P("row", None, None),
    )
    return jax.shard_map(
        per_device,
        mesh=mesh,
        in_specs=placed,
        out_specs=(
            P("row", None, None),
            P("row", None, None),
            P("row", "col", None, None),
            P("row", "col", None, None),
        ),
        check_vma=False,
    )
```

```python
import jax
import jax.numpy as jnp
from jax import lax
from jax.experimental import pallas as pl
from jax.experimental.pallas import tpu as pltpu
from jax.sharding import PartitionSpec as P

F32 = jnp.float32
BF16 = jnp.bfloat16
BLOCK = 64
WIDTH = 192
ONE = 16
TWO = 6
OWN = 3
COLS = 16
ROWS = 8
SLICE = 4
UNITS = [(k, m) for k in range(TWO) for m in range(k + 1)]
CHILD_ROWS = len(UNITS) * SLICE
BAND = ONE * SLICE
MESSAGE = 280
WIDE = TWO * BLOCK
VMEM = pl.BlockSpec(memory_space=pltpu.VMEM)
SMEM = pl.BlockSpec(memory_space=pltpu.SMEM)
ANY = pl.BlockSpec(memory_space=pl.ANY)


def split(value):
    high = value.astype(BF16)
    low = (value - high.astype(F32)).astype(BF16)
    return high, low


def product(left, right, dims=((1,), (0,))):
    def one(a, b):
        return lax.dot_general(a, b, (dims, ((), ())), preferred_element_type=F32)

    (lh, ll), (rh, rl) = left, right
    return one(lh, rh) + (one(lh, rl) + one(ll, rh))


def pack_kernel(root_ref, out_ref):
    for place in range(COLS):
        for n in range(8):
            out_ref[place, n] = root_ref[pl.ds(BLOCK * n + place, SLICE, stride=16), :]


def pack(root):
    return pl.pallas_call(
        pack_kernel,
        grid=(2,),
        out_shape=jax.ShapeDtypeStruct((COLS, 8, SLICE, 256), F32),
        in_specs=[pl.BlockSpec((512, 128), lambda tile: (0, tile))],
        out_specs=pl.BlockSpec((COLS, 8, SLICE, 128), lambda tile: (0, 0, 0, tile)),
        name="pack",
    )(root)


def select_kernel(core_ref, one_ref, two_ref, factor_ref, mine_ref, other_ref, out_ref, band):
    left_half = lax.broadcasted_iota(jnp.int32, (SLICE, 128), 1) < BLOCK
    core = core_ref[0]

    def row_step(a, carry):
        for parent in range(2):
            block = one_ref[parent, a]
            chip, row = block >> 4, block & 7
            is_mine = ((block >> 3) & 1) == core
            for pair in range(ONE // 2):
                halves = []
                for side in range(2):
                    block = one_ref[parent, 2 * pair + side]
                    lanes = pl.ds(pl.multiple_of(((block >> 1) & 1) << 7, 128), 128)
                    value = jnp.where(
                        is_mine,
                        mine_ref[chip, block >> 2, row, :, lanes],
                        other_ref[chip, block >> 2, row, :, lanes],
                    )
                    halves.append(pltpu.roll(value, ((block & 1) ^ side) << 6, 1))
                value = jnp.where(left_half, halves[0], halves[1])
                lanes = slice(pair * 128, pair * 128 + 128)
                band[0, parent, a, :, lanes] = value
                band[1, parent, a, :, lanes] = pltpu.roll(value, BLOCK, 1)
        return carry

    lax.fori_loop(0, ONE, row_step, 0)
    columns = jnp.concatenate(
        [
            -product(
                split(band[0, parent].reshape(BAND, ONE * BLOCK)),
                split(factor_ref[parent]),
                ((1,), (1,)),
            )
            for parent in range(2)
        ],
        axis=1,
    )
    for child in range(COLS):
        for tile in range(3):
            top = CHILD_ROWS + tile * BAND
            out_ref[child, top : top + BAND, :] = columns[:, 128 * tile : 128 * tile + 128]

    def child_step(child, carry):
        picks = [
            [jnp.maximum(two_ref[parent, child, n] - OWN, 0) for n in range(TWO)]
            for parent in range(2)
        ]
        for unit, (k, m) in enumerate(UNITS):
            halves = []
            for parent in range(2):
                block = picks[parent][m]
                lanes = pl.ds(pl.multiple_of((block >> 1) << 7, 128), 128)
                halves.append(band[(block & 1) ^ parent, parent, picks[parent][k], :, lanes])
            out_ref[child, unit * SLICE : unit * SLICE + SLICE, :] = jnp.where(
                left_half, halves[0], halves[1]
            )
        return carry

    lax.fori_loop(0, COLS, child_step, 0)


def select(core, pattern_one, pattern_two, factor, mine, other):
    return pl.pallas_call(
        select_kernel,
        out_shape=jax.ShapeDtypeStruct((COLS, MESSAGE, 128), F32),
        in_specs=[SMEM, SMEM, SMEM, VMEM, VMEM, VMEM],
        out_specs=VMEM,
        scratch_shapes=[pltpu.VMEM((2, 2, ONE, SLICE, ONE * BLOCK), F32)],
        compiler_params=pltpu.CompilerParams(vmem_limit_bytes=40 * 2**20),
        name="select",
    )(core, pattern_one, pattern_two, factor, mine, other)


def final_kernel(
    two_ref, got_ref, factor_ref, pivot_ref, child_factor_ref, child_pivot_ref,
    column_ref, diagonal_ref, child_column_ref, child_diagonal_ref, column, chosen,
):
    left_half = lax.broadcasted_iota(jnp.int32, (16, 128), 1) < BLOCK
    left_factor = lax.broadcasted_iota(jnp.int32, (WIDTH, 128), 1) < BLOCK
    nt = ((1,), (1,))
    for n in range(BAND):
        tiles = [
            got_ref[pl.ds(CHILD_ROWS + m * BAND + n, 16, stride=MESSAGE), :] for m in range(3)
        ]
        here = slice(16 * n, 16 * n + 16)
        column[0, here, 0:128] = tiles[0]
        column[0, here, 128:192] = tiles[1][:, :64]
        turned = [pltpu.roll(tile, BLOCK, 1) for tile in tiles[1:]]
        column[1, here, 0:128] = jnp.where(left_half, turned[0], turned[1])
        column[1, here, 128:192] = turned[1][:, :64]
    for unit, (k, m) in enumerate(UNITS):
        for n in range(SLICE):
            value = got_ref[pl.ds(unit * SLICE + n, 16, stride=MESSAGE), :]
            turned = pltpu.roll(value, BLOCK, 1)
            here = slice(BLOCK * k + 16 * n, BLOCK * k + 16 * n + 16)
            if m % 2 == 0:
                chosen[0, here, BLOCK * m : BLOCK * m + BLOCK] = value[:, :64]
                chosen[1, here, BLOCK * m : BLOCK * m + BLOCK] = turned[:, :64]
            else:
                chosen[0, here, BLOCK * m : BLOCK * m + BLOCK] = turned[:, 64:]
                chosen[1, here, BLOCK * m : BLOCK * m + BLOCK] = value[:, 64:]
    row_block = lax.broadcasted_iota(jnp.int32, (WIDE, WIDE), 0) // BLOCK
    lane_block = lax.broadcasted_iota(jnp.int32, (WIDE, WIDE), 1) // BLOCK
    for parent in range(2):
        column_ref[parent] = column[parent].T
        diagonal = pivot_ref[parent] - product(
            split(factor_ref[parent]), split(column[parent])
        )
        diagonal_ref[parent] = diagonal
        picks = [two_ref[parent, n] for n in range(TWO)]
        factor = child_factor_ref[parent, 0]
        tiles = [factor[:, 128 * n : 128 * n + 128] for n in range(TWO // 2)]
        kept = [picks[n] >= OWN for n in range(TWO)]
        outside = jnp.concatenate(
            [
                jnp.where(
                    left_factor,
                    jnp.where(kept[2 * n], tiles[n], 0.0),
                    jnp.where(kept[2 * n + 1], tiles[n], 0.0),
                )
                for n in range(TWO // 2)
            ],
            axis=1,
        )
        turned = pltpu.roll(tiles[0], BLOCK, 1)
        first = jnp.where(
            left_factor,
            jnp.where(picks[0] == 0, tiles[0], 0.0),
            jnp.where(picks[0] == 1, turned, 0.0) + jnp.where(picks[1] == 1, tiles[0], 0.0),
        )
        second = (
            jnp.where(picks[0] == 2, tiles[0], 0.0)
            + jnp.where(picks[1] == 2, turned, 0.0)
            + jnp.where(picks[2] == 2, tiles[1], 0.0)
        )
        inside = jnp.concatenate([first, second[:, :BLOCK]], axis=1)
        below = jnp.concatenate(
            [
                column[
                    parent,
                    pl.ds(pl.multiple_of(jnp.maximum(picks[n] - OWN, 0) << 6, BLOCK), BLOCK),
                    :,
                ]
                for n in range(TWO)
            ],
            axis=0,
        )
        lower = jnp.where(row_block >= lane_block, chosen[parent], 0.0)
        strict = jnp.where(row_block > lane_block, chosen[parent], 0.0)
        outside, inside, below = split(outside), split(inside), split(below)
        far = (
            product(outside, split(lower))
            + product(outside, split(strict), nt)
            + product(inside, below, nt)
        )
        near = product(inside, split(diagonal)) + product(outside, below)
        near = jnp.concatenate([near, jnp.zeros((WIDTH, BLOCK), F32)], axis=1)
        near_tiles = [near[:, 0:128], near[:, 128:256]]
        near_turned = [pltpu.roll(tile, BLOCK, 1) for tile in near_tiles]
        far_tiles = [far[:, 128 * n : 128 * n + 128] for n in range(TWO // 2)]
        even = jnp.where(
            kept[0],
            far_tiles[0],
            jnp.where(
                picks[0] == 0,
                near_tiles[0],
                jnp.where(picks[0] == 1, near_turned[0], near_tiles[1]),
            ),
        )
        odd = jnp.where(
            kept[1], far_tiles[0], jnp.where(picks[1] == 1, near_tiles[0], near_turned[1])
        )
        third = jnp.where(left_factor & jnp.logical_not(kept[2]), near_tiles[1], far_tiles[1])
        result = -jnp.concatenate(
            [jnp.where(left_factor, even, odd), third, far_tiles[2]], axis=1
        )
        child_column_ref[parent, 0] = result
        child_diagonal_ref[parent, 0] = child_pivot_ref[parent, 0] - product(
            split(factor), split(result), nt
        )


def finish(own_two, got, factor, pivot, child_factor, child_pivot):
    return pl.pallas_call(
        final_kernel,
        out_shape=(
            jax.ShapeDtypeStruct((2, WIDTH, ONE * BLOCK), F32),
            jax.ShapeDtypeStruct((2, WIDTH, WIDTH), F32),
            jax.ShapeDtypeStruct((2, 1, WIDTH, WIDE), F32),
            jax.ShapeDtypeStruct((2, 1, WIDTH, WIDTH), F32),
        ),
        in_specs=[SMEM] + [VMEM] * 5,
        out_specs=(VMEM,) * 4,
        scratch_shapes=[
            pltpu.VMEM((2, ONE * BLOCK, WIDTH), F32),
            pltpu.VMEM((2, WIDE, WIDE), F32),
        ],
        compiler_params=pltpu.CompilerParams(vmem_limit_bytes=40 * 2**20),
        name="finish",
    )(own_two, got, factor, pivot, child_factor, child_pivot)


CHIPS = [list(range(core, ROWS, 2)) for core in range(2)]
SWAP = [(r, r ^ 1) for r in range(ROWS)]


def per_device(
    root_inverse, factor_one, pivot_one, pattern_one, factor_two, pivot_two, pattern_two
):
    core = (lax.axis_index("row") & 1).astype(jnp.int32).reshape(1)
    col = lax.axis_index("col")
    factor_one = jnp.swapaxes(factor_one, 1, 2)
    factor_two = jnp.swapaxes(factor_two, 2, 3)
    shard = lax.all_to_all(pack(root_inverse), "col", 0, 0, tiled=True)
    copies = jnp.broadcast_to(shard[None], (4,) + shard.shape)
    mine = lax.all_to_all(copies, "row", 0, 0, axis_index_groups=CHIPS, tiled=True)
    other = lax.ppermute(mine, "row", SWAP)
    message = select(core, pattern_one, pattern_two, factor_one, mine, other)
    got = lax.all_to_all(message, "col", 0, 0, tiled=True)
    own_two = lax.dynamic_index_in_dim(pattern_two, col, 1, keepdims=False)
    column_one, diagonal_one, column_two, diagonal_two = finish(
        own_two, got.reshape(COLS * MESSAGE, 128), factor_one, pivot_one, factor_two, pivot_two
    )
    return (
        jnp.swapaxes(column_one, 1, 2),
        diagonal_one,
        jnp.swapaxes(column_two, 2, 3),
        diagonal_two,
    )


def solution(mesh):
    placed = (
        P("row", "col"),
        P("row", None, None),
        P("row", None, None),
        P("row", None),
        P("row", "col", None, None),
        P("row", "col", None, None),
        P("row", None, None),
    )
    return jax.shard_map(
        per_device,
        mesh=mesh,
        in_specs=placed,
        out_specs=(
            P("row", None, None),
            P("row", None, None),
            P("row", "col", None, None),
            P("row", "col", None, None),
        ),
        check_vma=False,
    )
```

```python
import jax
import jax.numpy as jnp
from jax import lax
from jax.experimental import pallas as pl
from jax.experimental.pallas import tpu as pltpu
from jax.sharding import PartitionSpec as P

F32 = jnp.float32
BF16 = jnp.bfloat16
BLOCK = 64
WIDTH = 192
ONE = 16
TWO = 6
OWN = 3
COLS = 16
ROWS = 8
SLICE = 4
UNITS = [(k, m) for k in range(TWO) for m in range(k + 1)]
CHILD_ROWS = len(UNITS) * SLICE
BAND = ONE * SLICE
MESSAGE = 280
WIDE = TWO * BLOCK
VMEM = pl.BlockSpec(memory_space=pltpu.VMEM)
SMEM = pl.BlockSpec(memory_space=pltpu.SMEM)
ANY = pl.BlockSpec(memory_space=pl.ANY)


def split(value):
    high = value.astype(BF16)
    low = (value - high.astype(F32)).astype(BF16)
    return high, low


def product(left, right, dims=((1,), (0,))):
    def one(a, b):
        return lax.dot_general(a, b, (dims, ((), ())), preferred_element_type=F32)

    (lh, ll), (rh, rl) = left, right
    return one(lh, rh) + (one(lh, rl) + one(ll, rh))


def pack_kernel(root_ref, out_ref):
    for place in range(COLS):
        for n in range(8):
            out_ref[place, n] = root_ref[pl.ds(BLOCK * n + place, SLICE, stride=16), :]


def pack(root):
    return pl.pallas_call(
        pack_kernel,
        grid=(2,),
        out_shape=jax.ShapeDtypeStruct((COLS, 8, SLICE, 256), F32),
        in_specs=[pl.BlockSpec((512, 128), lambda tile: (0, tile))],
        out_specs=pl.BlockSpec((COLS, 8, SLICE, 128), lambda tile: (0, 0, 0, tile)),
        name="pack",
    )(root)


def select_kernel(place_ref, one_ref, two_ref, factor_ref, *refs):
    pieces, (out_ref, rows, band, ready, sems) = refs[:10], refs[10:]
    left_half = lax.broadcasted_iota(jnp.int32, (ONE, SLICE, 128), 2) < BLOCK
    chip, core = place_ref[0], place_ref[1]

    def row_step(a, carry):
        for parent in range(2):
            block = one_ref[parent, a]
            step = ((block >> 4) - chip) & 3
            source = 2 * step + (((block >> 3) & 1) ^ core)
            row = block & 7

            def copy_row(piece, start):
                rows[parent, a] = piece[:, row - start]

            for side in range(2):
                own, ahead, behind, low, high = pieces[side::2]

                @pl.when(source == side)
                def _():
                    copy_row(own, 0)

                @pl.when(source == 2 + side)
                def _():
                    copy_row(ahead, 0)

                @pl.when(source == 6 + side)
                def _():
                    copy_row(behind, 0)

                @pl.when((source == 4 + side) & (row < 4))
                def _():
                    copy_row(low, 0)

                @pl.when((source == 4 + side) & (row >= 4))
                def _():
                    copy_row(high, 4)

        return carry

    lax.fori_loop(0, ONE, row_step, 0)
    for parent in range(2):
        for pair in range(ONE // 2):
            halves = []
            for side in range(2):
                block = one_ref[parent, 2 * pair + side]
                lanes = pl.ds(pl.multiple_of(((block >> 1) & 1) << 7, 128), 128)
                value = rows[parent, :, block >> 2, :, lanes]
                halves.append(pltpu.roll(value, ((block & 1) ^ side) << 6, 2))
            value = jnp.where(left_half, halves[0], halves[1])
            lanes = slice(pair * 128, pair * 128 + 128)
            band[0, parent, :, :, lanes] = value
            band[1, parent, :, :, lanes] = pltpu.roll(value, BLOCK, 2)
    columns = jnp.concatenate(
        [
            -product(
                split(band[0, parent].reshape(BAND, ONE * BLOCK)),
                split(factor_ref[parent]),
                ((1,), (1,)),
            )
            for parent in range(2)
        ],
        axis=1,
    )
    for child in range(COLS):
        for tile in range(3):
            top = CHILD_ROWS + tile * BAND
            ready[child, top : top + BAND, :] = columns[:, 128 * tile : 128 * tile + 128]
    left_half = lax.broadcasted_iota(jnp.int32, (SLICE, 128), 1) < BLOCK

    def send(child):
        return pltpu.make_async_copy(ready.at[child], out_ref.at[child], sems.at[child])

    def child_step(child, carry):
        picks = [
            [jnp.maximum(two_ref[parent, child, n] - OWN, 0) for n in range(TWO)]
            for parent in range(2)
        ]
        for unit, (k, m) in enumerate(UNITS):
            halves = []
            for parent in range(2):
                block = picks[parent][m]
                lanes = pl.ds(pl.multiple_of((block >> 1) << 7, 128), 128)
                halves.append(band[(block & 1) ^ parent, parent, picks[parent][k], :, lanes])
            ready[child, unit * SLICE : unit * SLICE + SLICE, :] = jnp.where(
                left_half, halves[0], halves[1]
            )
        send(child).start()
        return carry

    lax.fori_loop(0, COLS, child_step, 0)
    for child in range(COLS):
        send(child).wait()


def select(place, pattern_one, pattern_two, factor, pieces):
    return pl.pallas_call(
        select_kernel,
        out_shape=jax.ShapeDtypeStruct((COLS, MESSAGE, 128), F32),
        in_specs=[SMEM, SMEM, SMEM] + [VMEM] * 11,
        out_specs=pl.BlockSpec(memory_space=pltpu.HBM),
        scratch_shapes=[
            pltpu.VMEM((2, ONE, COLS, SLICE, 256), F32),
            pltpu.VMEM((2, 2, ONE, SLICE, ONE * BLOCK), F32),
            pltpu.VMEM((COLS, MESSAGE, 128), F32),
            pltpu.SemaphoreType.DMA((COLS,)),
        ],
        compiler_params=pltpu.CompilerParams(vmem_limit_bytes=20 * 2**20),
        name="select",
    )(place, pattern_one, pattern_two, factor, *pieces)


def final_kernel(
    two_ref, far_ref, factor_ref, pivot_ref, child_factor_ref, child_pivot_ref,
    column_ref, diagonal_ref, child_column_ref, child_diagonal_ref, got_ref, column, chosen, sems,
):
    fetch = pltpu.make_async_copy(far_ref, got_ref, sems.at[0])
    fetch.start()
    fetch.wait()
    left_half = lax.broadcasted_iota(jnp.int32, (16, 128), 1) < BLOCK
    left_factor = lax.broadcasted_iota(jnp.int32, (WIDTH, 128), 1) < BLOCK
    nt = ((1,), (1,))
    for n in range(BAND):
        tiles = [
            got_ref[pl.ds(CHILD_ROWS + m * BAND + n, 16, stride=MESSAGE), :] for m in range(3)
        ]
        here = slice(16 * n, 16 * n + 16)
        column[0, here, 0:128] = tiles[0]
        column[0, here, 128:192] = tiles[1][:, :64]
        turned = [pltpu.roll(tile, BLOCK, 1) for tile in tiles[1:]]
        column[1, here, 0:128] = jnp.where(left_half, turned[0], turned[1])
        column[1, here, 128:192] = turned[1][:, :64]
    for unit, (k, m) in enumerate(UNITS):
        for n in range(SLICE):
            value = got_ref[pl.ds(unit * SLICE + n, 16, stride=MESSAGE), :]
            turned = pltpu.roll(value, BLOCK, 1)
            here = slice(BLOCK * k + 16 * n, BLOCK * k + 16 * n + 16)
            if m % 2 == 0:
                chosen[0, here, BLOCK * m : BLOCK * m + BLOCK] = value[:, :64]
                chosen[1, here, BLOCK * m : BLOCK * m + BLOCK] = turned[:, :64]
            else:
                chosen[0, here, BLOCK * m : BLOCK * m + BLOCK] = turned[:, 64:]
                chosen[1, here, BLOCK * m : BLOCK * m + BLOCK] = value[:, 64:]
    row_block = lax.broadcasted_iota(jnp.int32, (WIDE, WIDE), 0) // BLOCK
    lane_block = lax.broadcasted_iota(jnp.int32, (WIDE, WIDE), 1) // BLOCK
    for parent in range(2):
        column_ref[parent] = column[parent].T
        diagonal = pivot_ref[parent] - product(
            split(factor_ref[parent]), split(column[parent])
        )
        diagonal_ref[parent] = diagonal
        picks = [two_ref[parent, n] for n in range(TWO)]
        factor = child_factor_ref[parent, 0]
        tiles = [factor[:, 128 * n : 128 * n + 128] for n in range(TWO // 2)]
        kept = [picks[n] >= OWN for n in range(TWO)]
        outside = jnp.concatenate(
            [
                jnp.where(
                    left_factor,
                    jnp.where(kept[2 * n], tiles[n], 0.0),
                    jnp.where(kept[2 * n + 1], tiles[n], 0.0),
                )
                for n in range(TWO // 2)
            ],
            axis=1,
        )
        turned = pltpu.roll(tiles[0], BLOCK, 1)
        first = jnp.where(
            left_factor,
            jnp.where(picks[0] == 0, tiles[0], 0.0),
            jnp.where(picks[0] == 1, turned, 0.0) + jnp.where(picks[1] == 1, tiles[0], 0.0),
        )
        second = (
            jnp.where(picks[0] == 2, tiles[0], 0.0)
            + jnp.where(picks[1] == 2, turned, 0.0)
            + jnp.where(picks[2] == 2, tiles[1], 0.0)
        )
        inside = jnp.concatenate([first, second[:, :BLOCK]], axis=1)
        below = jnp.concatenate(
            [
                column[
                    parent,
                    pl.ds(pl.multiple_of(jnp.maximum(picks[n] - OWN, 0) << 6, BLOCK), BLOCK),
                    :,
                ]
                for n in range(TWO)
            ],
            axis=0,
        )
        lower = jnp.where(row_block >= lane_block, chosen[parent], 0.0)
        strict = jnp.where(row_block > lane_block, chosen[parent], 0.0)
        outside, inside, below = split(outside), split(inside), split(below)
        far = (
            product(outside, split(lower))
            + product(outside, split(strict), nt)
            + product(inside, below, nt)
        )
        near = product(inside, split(diagonal)) + product(outside, below)
        near = jnp.concatenate([near, jnp.zeros((WIDTH, BLOCK), F32)], axis=1)
        near_tiles = [near[:, 0:128], near[:, 128:256]]
        near_turned = [pltpu.roll(tile, BLOCK, 1) for tile in near_tiles]
        far_tiles = [far[:, 128 * n : 128 * n + 128] for n in range(TWO // 2)]
        even = jnp.where(
            kept[0],
            far_tiles[0],
            jnp.where(
                picks[0] == 0,
                near_tiles[0],
                jnp.where(picks[0] == 1, near_turned[0], near_tiles[1]),
            ),
        )
        odd = jnp.where(
            kept[1], far_tiles[0], jnp.where(picks[1] == 1, near_tiles[0], near_turned[1])
        )
        third = jnp.where(left_factor & jnp.logical_not(kept[2]), near_tiles[1], far_tiles[1])
        result = -jnp.concatenate(
            [jnp.where(left_factor, even, odd), third, far_tiles[2]], axis=1
        )
        child_column_ref[parent, 0] = result
        child_diagonal_ref[parent, 0] = child_pivot_ref[parent, 0] - product(
            split(factor), split(result), nt
        )


def finish(own_two, got, factor, pivot, child_factor, child_pivot):
    return pl.pallas_call(
        final_kernel,
        out_shape=(
            jax.ShapeDtypeStruct((2, WIDTH, ONE * BLOCK), F32),
            jax.ShapeDtypeStruct((2, WIDTH, WIDTH), F32),
            jax.ShapeDtypeStruct((2, 1, WIDTH, WIDE), F32),
            jax.ShapeDtypeStruct((2, 1, WIDTH, WIDTH), F32),
        ),
        in_specs=[SMEM, ANY] + [VMEM] * 4,
        out_specs=(VMEM,) * 4,
        scratch_shapes=[
            pltpu.VMEM((COLS * MESSAGE, 128), F32),
            pltpu.VMEM((2, ONE * BLOCK, WIDTH), F32),
            pltpu.VMEM((2, WIDE, WIDE), F32),
            pltpu.SemaphoreType.DMA((1,)),
        ],
        compiler_params=pltpu.CompilerParams(vmem_limit_bytes=24 * 2**20),
        name="finish",
    )(own_two, got, factor, pivot, child_factor, child_pivot)


FORWARD = [(r, (r + 2) % ROWS) for r in range(ROWS)]
BACKWARD = [(r, (r - 2) % ROWS) for r in range(ROWS)]
SWAP = [(r, r ^ 1) for r in range(ROWS)]


def per_device(
    root_inverse, factor_one, pivot_one, pattern_one, factor_two, pivot_two, pattern_two
):
    row = lax.axis_index("row")
    place = jnp.stack([row >> 1, row & 1]).astype(jnp.int32)
    col = lax.axis_index("col")
    factor_one = jnp.swapaxes(factor_one, 1, 2)
    factor_two = jnp.swapaxes(factor_two, 2, 3)
    shard = lax.all_to_all(pack(root_inverse), "col", 0, 0, tiled=True)
    behind = lax.ppermute(shard, "row", FORWARD)
    ahead = lax.ppermute(shard, "row", BACKWARD)
    low = lax.ppermute(behind[:, :4], "row", FORWARD)
    high = lax.ppermute(ahead[:, 4:], "row", BACKWARD)
    pieces = []
    for piece in (shard, ahead, behind, low, high):
        pieces += [piece, lax.ppermute(piece, "row", SWAP)]
    message = select(place, pattern_one, pattern_two, factor_one, pieces)
    got = lax.all_to_all(message, "col", 0, 0, tiled=True)
    own_two = lax.dynamic_index_in_dim(pattern_two, col, 1, keepdims=False)
    column_one, diagonal_one, column_two, diagonal_two = finish(
        own_two, got.reshape(COLS * MESSAGE, 128), factor_one, pivot_one, factor_two, pivot_two
    )
    return (
        jnp.swapaxes(column_one, 1, 2),
        diagonal_one,
        jnp.swapaxes(column_two, 2, 3),
        diagonal_two,
    )


def solution(mesh):
    placed = (
        P("row", "col"),
        P("row", None, None),
        P("row", None, None),
        P("row", None),
        P("row", "col", None, None),
        P("row", "col", None, None),
        P("row", None, None),
    )
    return jax.shard_map(
        per_device,
        mesh=mesh,
        in_specs=placed,
        out_specs=(
            P("row", None, None),
            P("row", None, None),
            P("row", "col", None, None),
            P("row", "col", None, None),
        ),
        check_vma=False,
    )
```

```python
import jax
import jax.numpy as jnp
from jax import lax
from jax.experimental import pallas as pl
from jax.experimental.pallas import tpu as pltpu
from jax.sharding import PartitionSpec as P

F32 = jnp.float32
BF16 = jnp.bfloat16
BLOCK = 64
WIDTH = 192
ONE = 16
TWO = 6
OWN = 3
COLS = 16
ROWS = 8
SLICE = 4
UNITS = [(k, m) for k in range(TWO) for m in range(k + 1)]
BAND = ONE * SLICE
CHILD_TOP = 3 * BAND
MESSAGE = 280
WIDE = TWO * BLOCK
VMEM = pl.BlockSpec(memory_space=pltpu.VMEM)
SMEM = pl.BlockSpec(memory_space=pltpu.SMEM)
ANY = pl.BlockSpec(memory_space=pl.ANY)


def split(value):
    high = value.astype(BF16)
    low = (value - high.astype(F32)).astype(BF16)
    return high, low


def product(left, right, dims=((1,), (0,))):
    def one(a, b):
        return lax.dot_general(a, b, (dims, ((), ())), preferred_element_type=F32)

    (lh, ll), (rh, rl) = left, right
    return one(lh, rh) + (one(lh, rl) + one(ll, rh))


def pack_kernel(root_ref, out_ref):
    for place in range(COLS):
        for n in range(8):
            out_ref[place, n] = root_ref[pl.ds(BLOCK * n + place, SLICE, stride=16), :]


def pack(root):
    return pl.pallas_call(
        pack_kernel,
        grid=(2,),
        out_shape=jax.ShapeDtypeStruct((COLS, 8, SLICE, 256), F32),
        in_specs=[pl.BlockSpec((512, 128), lambda tile: (0, tile))],
        out_specs=pl.BlockSpec((COLS, 8, SLICE, 128), lambda tile: (0, 0, 0, tile)),
        name="pack",
    )(root)


def pick_lanes(one_ref, parent, pair, side):
    block = one_ref[parent, 2 * pair + side]
    lanes = pl.ds(pl.multiple_of(((block >> 1) & 1) << 7, 128), 128)
    return block >> 2, lanes, ((block & 1) ^ side) << 6


def source_of(place_ref, block):
    return (((block >> 4) - place_ref[0]) & 3), ((block >> 3) & 1) ^ place_ref[1]


def early_kernel(place_ref, one_ref, *refs):
    pieces, (band, rows) = refs[:6], refs[6:]
    left_half = lax.broadcasted_iota(jnp.int32, (8, 8, 128), 2) < BLOCK

    def row_step(couple, carry):
        for parent in range(2):
            for odd in range(2):
                block = one_ref[parent, 2 * couple + odd]
                step, side = source_of(place_ref, block)
                for n, place in enumerate((0, 1, 3)):

                    @pl.when(step == place)
                    def _():
                        for other in range(2):

                            @pl.when(side == other)
                            def _():
                                rows[parent, couple, :, 4 * odd : 4 * odd + 4, :] = pieces[
                                    2 * n + other
                                ][:, block & 7]

        return carry

    lax.fori_loop(0, ONE // 2, row_step, 0)
    for parent in range(2):
        for pair in range(ONE // 2):
            halves = []
            for side in range(2):
                source, lanes, turn = pick_lanes(one_ref, parent, pair, side)
                halves.append(pltpu.roll(rows[parent, :, source, :, lanes], turn, 2))
            value = jnp.where(left_half, halves[0], halves[1])
            turned = pltpu.roll(value, BLOCK, 2)
            lanes = slice(pair * 128, pair * 128 + 128)
            for odd in range(2):
                band[0, parent, :, odd, :, lanes] = value[:, 4 * odd : 4 * odd + 4]
                band[1, parent, :, odd, :, lanes] = turned[:, 4 * odd : 4 * odd + 4]


BAND_SHAPE = (2, 2, ONE // 2, 2, SLICE, ONE * BLOCK)


def early(place, pattern_one, pieces):
    return pl.pallas_call(
        early_kernel,
        out_shape=jax.ShapeDtypeStruct(BAND_SHAPE, F32),
        in_specs=[SMEM, SMEM] + [VMEM] * 6,
        out_specs=VMEM,
        scratch_shapes=[pltpu.VMEM((2, ONE // 2, COLS, 8, 256), F32)],
        compiler_params=pltpu.CompilerParams(vmem_limit_bytes=20 * 2**20),
        cost_estimate=pl.CostEstimate(flops=0, bytes_accessed=12 * 2**20, transcendentals=0),
        name="early",
    )(place, pattern_one, *pieces)


def select_kernel(place_ref, one_ref, two_ref, factor_ref, early_ref, *refs):
    pieces, (out_ref, band, ready, sems) = refs[:4], refs[4:]
    left_half = lax.broadcasted_iota(jnp.int32, (SLICE, 128), 1) < BLOCK
    band[...] = early_ref[...]

    def row_step(couple, carry):
        for parent in range(2):
            for odd in range(2):
                block = one_ref[parent, 2 * couple + odd]
                step, side = source_of(place_ref, block)

                def fill(piece):
                    for pair in range(ONE // 2):
                        halves = []
                        for at in range(2):
                            source, lanes, turn = pick_lanes(one_ref, parent, pair, at)
                            halves.append(pltpu.roll(piece[source, block & 3, :, lanes], turn, 1))
                        value = jnp.where(left_half, halves[0], halves[1])
                        lanes = slice(pair * 128, pair * 128 + 128)
                        band[0, parent, couple, odd, :, lanes] = value
                        band[1, parent, couple, odd, :, lanes] = pltpu.roll(value, BLOCK, 1)

                @pl.when(step == 2)
                def _():
                    for high in range(2):
                        for other in range(2):

                            @pl.when((side == other) & (((block >> 2) & 1) == high))
                            def _():
                                fill(pieces[2 * high + other])

        return carry

    lax.fori_loop(0, ONE // 2, row_step, 0)
    columns = jnp.concatenate(
        [
            -product(
                split(band[0, parent].reshape(BAND, ONE * BLOCK)),
                split(factor_ref[parent]),
                ((1,), (1,)),
            )
            for parent in range(2)
        ],
        axis=1,
    )
    for child in range(COLS):
        for tile in range(3):
            ready[child, tile * BAND : tile * BAND + BAND, :] = columns[
                :, 128 * tile : 128 * tile + 128
            ]

    def send(n):
        children = slice(0, COLS) if n == 0 else slice(8 * (n - 1), 8 * n)
        part = slice(0, CHILD_TOP) if n == 0 else slice(CHILD_TOP, MESSAGE)
        return pltpu.make_async_copy(
            ready.at[children, part], out_ref.at[children, part], sems.at[n]
        )

    def child_step(child, carry):
        picks = [
            [jnp.maximum(two_ref[parent, child, n] - OWN, 0) for n in range(TWO)]
            for parent in range(2)
        ]
        for unit, (k, m) in enumerate(UNITS):
            halves = []
            for parent in range(2):
                row, block = picks[parent][k], picks[parent][m]
                lanes = pl.ds(pl.multiple_of((block >> 1) << 7, 128), 128)
                halves.append(band[(block & 1) ^ parent, parent, row >> 1, row & 1, :, lanes])
            top = CHILD_TOP + unit * SLICE
            ready[child, top : top + SLICE, :] = jnp.where(left_half, halves[0], halves[1])
        return carry

    send(0).start()
    lax.fori_loop(0, 8, child_step, 0)
    send(1).start()
    lax.fori_loop(8, COLS, child_step, 0)
    send(2).start()
    for n in range(3):
        send(n).wait()


def select(place, pattern_one, pattern_two, factor, band, pieces):
    return pl.pallas_call(
        select_kernel,
        out_shape=pltpu.HBM((COLS, MESSAGE, 128), F32),
        in_specs=[SMEM, SMEM, SMEM] + [VMEM] * 6,
        out_specs=pl.BlockSpec(memory_space=pltpu.HBM),
        scratch_shapes=[
            pltpu.VMEM(BAND_SHAPE, F32),
            pltpu.VMEM((COLS, MESSAGE, 128), F32),
            pltpu.SemaphoreType.DMA((3,)),
        ],
        compiler_params=pltpu.CompilerParams(vmem_limit_bytes=20 * 2**20),
        name="select",
    )(place, pattern_one, pattern_two, factor, band, *pieces)


def final_kernel(
    two_ref, got_ref, far_factor, far_pivot, far_child_factor, far_child_pivot,
    column_ref, diagonal_ref, child_column_ref, child_diagonal_ref,
    beside, chosen, factor_ref, pivot_ref, child_factor_ref, child_pivot_ref, sems,
):
    fetches = [
        pltpu.make_async_copy(far, near, sems.at[n])
        for n, (far, near) in enumerate(
            (
                (far_factor, factor_ref),
                (far_pivot, pivot_ref),
                (far_child_factor, child_factor_ref),
                (far_child_pivot, child_pivot_ref),
            )
        )
    ]
    for fetch in fetches:
        fetch.start()
    left_half = lax.broadcasted_iota(jnp.int32, (16, 128), 1) < BLOCK
    left_block = lax.broadcasted_iota(jnp.int32, (BLOCK, 128), 1) < BLOCK
    nt = ((1,), (1,))
    for n in range(BAND):
        tiles = [got_ref[pl.ds(m * BAND + n, 16, stride=MESSAGE), :] for m in range(3)]
        here = slice(WIDTH + 16 * n, WIDTH + 16 * n + 16)
        turned = [pltpu.roll(tile, BLOCK, 1) for tile in tiles[1:]]
        beside[0, here, 0:128] = tiles[0]
        beside[0, here, 128:256] = tiles[1]
        beside[1, here, 0:128] = jnp.where(left_half, turned[0], turned[1])
        beside[1, here, 128:256] = turned[1]
    for unit, (k, m) in enumerate(UNITS):
        for n in range(SLICE):
            value = got_ref[pl.ds(CHILD_TOP + unit * SLICE + n, 16, stride=MESSAGE), :]
            turned = pltpu.roll(value, BLOCK, 1)
            here = slice(BLOCK * k + 16 * n, BLOCK * k + 16 * n + 16)
            lanes = slice(BLOCK * m, BLOCK * m + BLOCK)
            half = slice(0, BLOCK) if m % 2 == 0 else slice(BLOCK, 128)
            chosen[m % 2, here, lanes] = value[:, half]
            chosen[1 - m % 2, here, lanes] = turned[:, half]
    row_block = lax.broadcasted_iota(jnp.int32, (WIDE, WIDE), 0) // BLOCK
    lane_block = lax.broadcasted_iota(jnp.int32, (WIDE, WIDE), 1) // BLOCK
    for fetch in fetches:
        fetch.wait()
    for parent in range(2):
        column = beside[parent, WIDTH:, 0:WIDTH]
        column_ref[parent] = column.T
        diagonal = pivot_ref[parent] - product(split(factor_ref[parent]), split(column))
        diagonal_ref[parent] = diagonal
        beside[parent, 0:WIDTH, 0:WIDTH] = diagonal
        picks = [two_ref[parent, n] for n in range(TWO)]
        for k in range(TWO):
            here = slice(BLOCK * k, BLOCK * k + BLOCK)
            start = pl.multiple_of(picks[k] << 6, BLOCK)
            tiles = [beside[parent, pl.ds(start, BLOCK), 128 * n : 128 * n + 128] for n in range(2)]
            turned = [pltpu.roll(tile, BLOCK, 1) for tile in tiles]
            even = jnp.where(
                picks[0] == 0, tiles[0], jnp.where(picks[0] == 1, turned[0], tiles[1])
            )
            odd = jnp.where(picks[1] == 1, tiles[0], turned[1])
            near = chosen[parent, here, 0:128]
            chosen[parent, here, 0:128] = jnp.where(
                left_block,
                jnp.where(picks[0] >= OWN, near, even),
                jnp.where(picks[1] >= OWN, near, odd),
            )
            if k >= 2:
                near = chosen[parent, here, 128:256]
                chosen[parent, here, 128:256] = jnp.where(
                    left_block & (picks[2] < OWN), tiles[1], near
                )
        lower = chosen[parent]
        whole = jnp.where(row_block >= lane_block, lower, lower.T)
        factor = split(child_factor_ref[parent, 0])
        result = -product(factor, split(whole))
        child_column_ref[parent, 0] = result
        child_diagonal_ref[parent, 0] = child_pivot_ref[parent, 0] - product(
            factor, split(result), nt
        )


def finish(own_two, got, factor, pivot, child_factor, child_pivot):
    arrays = (factor, pivot, child_factor, child_pivot)
    return pl.pallas_call(
        final_kernel,
        out_shape=(
            jax.ShapeDtypeStruct((2, WIDTH, ONE * BLOCK), F32),
            jax.ShapeDtypeStruct((2, WIDTH, WIDTH), F32),
            jax.ShapeDtypeStruct((2, 1, WIDTH, WIDE), F32),
            jax.ShapeDtypeStruct((2, 1, WIDTH, WIDTH), F32),
        ),
        in_specs=[SMEM, VMEM] + [pl.BlockSpec(memory_space=pltpu.HBM)] * 4,
        out_specs=(VMEM,) * 4,
        scratch_shapes=[
            pltpu.VMEM((2, WIDTH + ONE * BLOCK, 256), F32),
            pltpu.VMEM((2, WIDE, WIDE), F32),
        ]
        + [pltpu.VMEM(array.shape, F32) for array in arrays]
        + [pltpu.SemaphoreType.DMA((4,))],
        compiler_params=pltpu.CompilerParams(vmem_limit_bytes=24 * 2**20),
        name="finish",
    )(own_two, got, *[pltpu.with_memory_space_constraint(a, pltpu.HBM) for a in arrays])


FORWARD = [(r, (r + 2) % ROWS) for r in range(ROWS)]
BACKWARD = [(r, (r - 2) % ROWS) for r in range(ROWS)]
SWAP = [(r, r ^ 1) for r in range(ROWS)]


def per_device(
    root_inverse, factor_one, pivot_one, pattern_one, factor_two, pivot_two, pattern_two
):
    row = lax.axis_index("row")
    place = jnp.stack([row >> 1, row & 1]).astype(jnp.int32)
    col = lax.axis_index("col")
    factor_one = jnp.swapaxes(factor_one, 1, 2)
    factor_two = jnp.swapaxes(factor_two, 2, 3)
    shard = lax.all_to_all(pack(root_inverse), "col", 0, 0, tiled=True)
    behind = lax.ppermute(shard, "row", FORWARD)
    ahead = lax.ppermute(shard, "row", BACKWARD)
    low = lax.ppermute(behind[:, :4], "row", FORWARD)
    high = lax.ppermute(ahead[:, 4:], "row", BACKWARD)
    pieces = []
    for piece in (shard, ahead, behind, low, high):
        pieces += [piece, lax.ppermute(piece, "row", SWAP)]
    band = early(place, pattern_one, pieces[:6])
    message = select(place, pattern_one, pattern_two, factor_one, band, pieces[6:])
    got = lax.all_to_all(message, "col", 0, 0, tiled=True)
    own_two = lax.dynamic_index_in_dim(pattern_two, col, 1, keepdims=False)
    column_one, diagonal_one, column_two, diagonal_two = finish(
        own_two, got.reshape(COLS * MESSAGE, 128), factor_one, pivot_one, factor_two, pivot_two
    )
    return (
        jnp.swapaxes(column_one, 1, 2),
        diagonal_one,
        jnp.swapaxes(column_two, 2, 3),
        diagonal_two,
    )


def solution(mesh):
    placed = (
        P("row", "col"),
        P("row", None, None),
        P("row", None, None),
        P("row", None),
        P("row", "col", None, None),
        P("row", "col", None, None),
        P("row", None, None),
    )
    return jax.shard_map(
        per_device,
        mesh=mesh,
        in_specs=placed,
        out_specs=(
            P("row", None, None),
            P("row", None, None),
            P("row", "col", None, None),
            P("row", "col", None, None),
        ),
        check_vma=False,
    )
```

```python
import jax
import jax.numpy as jnp
from jax import lax
from jax.experimental import pallas as pl
from jax.experimental.pallas import tpu as pltpu
from jax.sharding import PartitionSpec as P

F32 = jnp.float32
BF16 = jnp.bfloat16
BLOCK = 64
WIDTH = 192
ONE = 16
TWO = 6
OWN = 3
COLS = 16
ROWS = 8
SLICE = 4
UNITS = [(k, m) for k in range(TWO) for m in range(k + 1)]
BAND = ONE * SLICE
CHILD_TOP = 3 * BAND
MESSAGE = 280
WIDE = TWO * BLOCK
VMEM = pl.BlockSpec(memory_space=pltpu.VMEM)
SMEM = pl.BlockSpec(memory_space=pltpu.SMEM)
ANY = pl.BlockSpec(memory_space=pl.ANY)


def split(value):
    high = value.astype(BF16)
    low = (value - high.astype(F32)).astype(BF16)
    return high, low


def product(left, right, dims=((1,), (0,))):
    def one(a, b):
        return lax.dot_general(a, b, (dims, ((), ())), preferred_element_type=F32)

    (lh, ll), (rh, rl) = left, right
    return one(lh, rh) + (one(lh, rl) + one(ll, rh))


def pack_kernel(root_ref, out_ref):
    for place in range(COLS):
        for n in range(8):
            out_ref[place, n] = root_ref[pl.ds(BLOCK * n + place, SLICE, stride=16), :]


def pack(root):
    return pl.pallas_call(
        pack_kernel,
        grid=(2,),
        out_shape=jax.ShapeDtypeStruct((COLS, 8, SLICE, 256), F32),
        in_specs=[pl.BlockSpec((512, 128), lambda tile: (0, tile))],
        out_specs=pl.BlockSpec((COLS, 8, SLICE, 128), lambda tile: (0, 0, 0, tile)),
        name="pack",
    )(root)


def prepare_kernel(factor_ref, child_ref, high_ref, low_ref, child_high_ref, child_low_ref):
    for parent in range(2):
        high_ref[parent], low_ref[parent] = split(factor_ref[parent])
        child_high_ref[parent, 0], child_low_ref[parent, 0] = split(child_ref[parent, 0])


def prepare(factor, child_factor):
    shapes = [jax.ShapeDtypeStruct(a.shape, BF16) for a in (factor, factor, child_factor, child_factor)]
    return pl.pallas_call(
        prepare_kernel,
        out_shape=tuple(shapes),
        in_specs=[VMEM] * 2,
        out_specs=(VMEM,) * 4,
        compiler_params=pltpu.CompilerParams(vmem_limit_bytes=20 * 2**20),
        cost_estimate=pl.CostEstimate(flops=0, bytes_accessed=5 * 2**20, transcendentals=0),
        name="prepare",
    )(factor, child_factor)


def pick_lanes(one_ref, parent, pair, side):
    block = one_ref[parent, 2 * pair + side]
    lanes = pl.ds(pl.multiple_of(((block >> 1) & 1) << 7, 128), 128)
    return block >> 2, lanes, ((block & 1) ^ side) << 6


def source_of(place_ref, block):
    return (((block >> 4) - place_ref[0]) & 3), ((block >> 3) & 1) ^ place_ref[1]


def early_kernel(place_ref, one_ref, *refs):
    pieces, (band, rows) = refs[:10], refs[10:]
    left_half = lax.broadcasted_iota(jnp.int32, (8, 8, 128), 2) < BLOCK

    def row_step(couple, carry):
        for parent in range(2):
            for odd in range(2):
                block = one_ref[parent, 2 * couple + odd]
                step, side = source_of(place_ref, block)
                high = (block >> 2) & 1
                here = slice(4 * odd, 4 * odd + 4)

                for other in range(2):

                    @pl.when((step == 0) & (side == other))
                    def _():
                        rows[parent, couple, :, here, :] = pieces[other][:, block & 7]

                for n, place in ((1, 1), (2, 3)):

                    @pl.when(step == place)
                    def _():
                        for other in range(2):
                            for half in range(2):

                                @pl.when((side == other) & (high == half))
                                def _():
                                    rows[parent, couple, :, here, :] = pieces[
                                        4 * n - 2 + 2 * half + other
                                    ][:, block & 3]

        return carry

    lax.fori_loop(0, ONE // 2, row_step, 0)
    for parent in range(2):
        for pair in range(ONE // 2):
            halves = []
            for side in range(2):
                source, lanes, turn = pick_lanes(one_ref, parent, pair, side)
                halves.append(pltpu.roll(rows[parent, :, source, :, lanes], turn, 2))
            value = jnp.where(left_half, halves[0], halves[1])
            turned = pltpu.roll(value, BLOCK, 2)
            lanes = slice(pair * 128, pair * 128 + 128)
            for odd in range(2):
                band[0, parent, :, odd, :, lanes] = value[:, 4 * odd : 4 * odd + 4]
                band[1, parent, :, odd, :, lanes] = turned[:, 4 * odd : 4 * odd + 4]


BAND_SHAPE = (2, 2, ONE // 2, 2, SLICE, ONE * BLOCK)


def early(place, pattern_one, pieces):
    return pl.pallas_call(
        early_kernel,
        out_shape=jax.ShapeDtypeStruct(BAND_SHAPE, F32),
        in_specs=[SMEM, SMEM] + [VMEM] * 10,
        out_specs=VMEM,
        scratch_shapes=[pltpu.VMEM((2, ONE // 2, COLS, 8, 256), F32)],
        compiler_params=pltpu.CompilerParams(vmem_limit_bytes=20 * 2**20),
        cost_estimate=pl.CostEstimate(flops=0, bytes_accessed=12 * 2**20, transcendentals=0),
        name="early",
    )(place, pattern_one, *pieces)


def select_kernel(place_ref, one_ref, two_ref, high_ref, low_ref, early_ref, *refs):
    pieces, (out_ref, band, ready, sems) = refs[:4], refs[4:]
    left_half = lax.broadcasted_iota(jnp.int32, (SLICE, 128), 1) < BLOCK
    band[...] = early_ref[...]

    def row_step(couple, carry):
        for parent in range(2):
            for odd in range(2):
                block = one_ref[parent, 2 * couple + odd]
                step, side = source_of(place_ref, block)

                def fill(piece):
                    for pair in range(ONE // 2):
                        halves = []
                        for at in range(2):
                            source, lanes, turn = pick_lanes(one_ref, parent, pair, at)
                            halves.append(pltpu.roll(piece[source, block & 3, :, lanes], turn, 1))
                        value = jnp.where(left_half, halves[0], halves[1])
                        lanes = slice(pair * 128, pair * 128 + 128)
                        band[0, parent, couple, odd, :, lanes] = value
                        band[1, parent, couple, odd, :, lanes] = pltpu.roll(value, BLOCK, 1)

                @pl.when(step == 2)
                def _():
                    for high in range(2):
                        for other in range(2):

                            @pl.when((side == other) & (((block >> 2) & 1) == high))
                            def _():
                                fill(pieces[2 * high + other])

        return carry

    lax.fori_loop(0, ONE // 2, row_step, 0)
    columns = jnp.concatenate(
        [
            -product(
                split(band[0, parent].reshape(BAND, ONE * BLOCK)),
                (high_ref[parent], low_ref[parent]),
                ((1,), (1,)),
            )
            for parent in range(2)
        ],
        axis=1,
    )
    for child in range(COLS):
        for tile in range(3):
            ready[child, tile * BAND : tile * BAND + BAND, :] = columns[
                :, 128 * tile : 128 * tile + 128
            ]

    def send(n):
        children = slice(0, COLS) if n == 0 else slice(8 * (n - 1), 8 * n)
        part = slice(0, CHILD_TOP) if n == 0 else slice(CHILD_TOP, MESSAGE)
        return pltpu.make_async_copy(
            ready.at[children, part], out_ref.at[children, part], sems.at[n]
        )

    def child_step(child, carry):
        picks = [
            [jnp.maximum(two_ref[parent, child, n] - OWN, 0) for n in range(TWO)]
            for parent in range(2)
        ]
        for unit, (k, m) in enumerate(UNITS):
            halves = []
            for parent in range(2):
                row, block = picks[parent][k], picks[parent][m]
                lanes = pl.ds(pl.multiple_of((block >> 1) << 7, 128), 128)
                halves.append(band[(block & 1) ^ parent, parent, row >> 1, row & 1, :, lanes])
            top = CHILD_TOP + unit * SLICE
            ready[child, top : top + SLICE, :] = jnp.where(left_half, halves[0], halves[1])
        return carry

    send(0).start()
    lax.fori_loop(0, 8, child_step, 0)
    send(1).start()
    lax.fori_loop(8, COLS, child_step, 0)
    send(2).start()
    for n in range(3):
        send(n).wait()


def select(place, pattern_one, pattern_two, high, low, band, pieces):
    return pl.pallas_call(
        select_kernel,
        out_shape=pltpu.HBM((COLS, MESSAGE, 128), F32),
        in_specs=[SMEM, SMEM, SMEM] + [VMEM] * 7,
        out_specs=pl.BlockSpec(memory_space=pltpu.HBM),
        scratch_shapes=[
            pltpu.VMEM(BAND_SHAPE, F32),
            pltpu.VMEM((COLS, MESSAGE, 128), F32),
            pltpu.SemaphoreType.DMA((3,)),
        ],
        compiler_params=pltpu.CompilerParams(vmem_limit_bytes=20 * 2**20),
        name="select",
    )(place, pattern_one, pattern_two, high, low, band, *pieces)


def final_kernel(two_ref, got_ref, *refs):
    (far_in, far_out, beside, chosen, near_in, near_out, sems) = (
        refs[:6], refs[6:10], refs[10:12], refs[12:14], refs[14:20], refs[20:24], refs[24],
    )
    high_ref, low_ref, child_high_ref, child_low_ref, pivot_ref, child_pivot_ref = near_in
    column_ref, diagonal_ref, child_column_ref, child_diagonal_ref = near_out
    fetches = [
        pltpu.make_async_copy(far, near, sems.at[n])
        for n, (far, near) in enumerate(zip(far_in, near_in))
    ]
    stores = [
        [
            pltpu.make_async_copy(near.at[parent], far.at[parent], sems.at[6 + 2 * n + parent])
            for parent in range(2)
        ]
        for n, (far, near) in enumerate(zip(far_out, near_out))
    ]
    for fetch in fetches:
        fetch.start()
    left_half = lax.broadcasted_iota(jnp.int32, (16, 128), 1) < BLOCK
    left_block = lax.broadcasted_iota(jnp.int32, (BLOCK, 128), 1) < BLOCK
    nt = ((1,), (1,))
    for n in range(BAND):
        tiles = [got_ref[pl.ds(m * BAND + n, 16, stride=MESSAGE), :] for m in range(3)]
        here = slice(WIDTH + 16 * n, WIDTH + 16 * n + 16)
        turned = [pltpu.roll(tile, BLOCK, 1) for tile in tiles[1:]]
        beside[0][here, 0:128] = tiles[0]
        beside[0][here, 128:256] = tiles[1]
        beside[1][here, 0:128] = jnp.where(left_half, turned[0], turned[1])
        beside[1][here, 128:256] = turned[1]
    for parent in range(2):
        column_ref[parent] = beside[parent][WIDTH:, 0:WIDTH].T
        stores[0][parent].start()
    for fetch in fetches:
        fetch.wait()
    for parent in range(2):
        diagonal = pivot_ref[parent] - product(
            (high_ref[parent], low_ref[parent]), split(beside[parent][WIDTH:, 0:WIDTH])
        )
        diagonal_ref[parent] = diagonal
        beside[parent][0:WIDTH, 0:WIDTH] = diagonal
        stores[1][parent].start()
    for unit, (k, m) in enumerate(UNITS):
        for n in range(SLICE):
            value = got_ref[pl.ds(CHILD_TOP + unit * SLICE + n, 16, stride=MESSAGE), :]
            turned = pltpu.roll(value, BLOCK, 1)
            here = slice(BLOCK * k + 16 * n, BLOCK * k + 16 * n + 16)
            lanes = slice(BLOCK * m, BLOCK * m + BLOCK)
            half = slice(0, BLOCK) if m % 2 == 0 else slice(BLOCK, 128)
            chosen[m % 2][here, lanes] = value[:, half]
            chosen[1 - m % 2][here, lanes] = turned[:, half]
    row_block = lax.broadcasted_iota(jnp.int32, (WIDE, WIDE), 0) // BLOCK
    lane_block = lax.broadcasted_iota(jnp.int32, (WIDE, WIDE), 1) // BLOCK
    for parent in range(2):
        picks = [two_ref[parent, n] for n in range(TWO)]
        for k in range(TWO):
            here = slice(BLOCK * k, BLOCK * k + BLOCK)
            rows = pl.ds(pl.multiple_of(picks[k] << 6, BLOCK), BLOCK)
            tiles = [beside[parent][rows, 128 * n : 128 * n + 128] for n in range(2)]
            turned = [pltpu.roll(tile, BLOCK, 1) for tile in tiles]
            even = jnp.where(
                picks[0] == 0, tiles[0], jnp.where(picks[0] == 1, turned[0], tiles[1])
            )
            odd = jnp.where(picks[1] == 1, tiles[0], turned[1])
            near = chosen[parent][here, 0:128]
            chosen[parent][here, 0:128] = jnp.where(
                left_block,
                jnp.where(picks[0] >= OWN, near, even),
                jnp.where(picks[1] >= OWN, near, odd),
            )
            if k >= 2:
                near = chosen[parent][here, 128:256]
                chosen[parent][here, 128:256] = jnp.where(
                    left_block & (picks[2] < OWN), tiles[1], near
                )
    factors = [(child_high_ref[parent, 0], child_low_ref[parent, 0]) for parent in range(2)]
    results = []
    for parent in range(2):
        lower = chosen[parent][...]
        whole = jnp.where(row_block >= lane_block, lower, lower.T)
        results.append(-product(factors[parent], split(whole)))
    for parent in range(2):
        child_column_ref[parent, 0] = results[parent]
        stores[2][parent].start()
    for parent in range(2):
        child_diagonal_ref[parent, 0] = child_pivot_ref[parent, 0] - product(
            factors[parent], split(results[parent]), nt
        )
        stores[3][parent].start()
    for pair in stores:
        for store in pair:
            store.wait()


def finish(own_two, got, arrays):
    hbm = pl.BlockSpec(memory_space=pltpu.HBM)
    shapes = (
        (2, WIDTH, ONE * BLOCK),
        (2, WIDTH, WIDTH),
        (2, 1, WIDTH, WIDE),
        (2, 1, WIDTH, WIDTH),
    )
    return pl.pallas_call(
        final_kernel,
        out_shape=tuple(pltpu.HBM(shape, F32) for shape in shapes),
        in_specs=[SMEM, VMEM] + [hbm] * 6,
        out_specs=(hbm,) * 4,
        scratch_shapes=[pltpu.VMEM((WIDTH + ONE * BLOCK, 256), F32)] * 2
        + [pltpu.VMEM((WIDE, WIDE), F32)] * 2
        + [pltpu.VMEM(array.shape, array.dtype) for array in arrays]
        + [pltpu.VMEM(shape, F32) for shape in shapes]
        + [pltpu.SemaphoreType.DMA((14,))],
        compiler_params=pltpu.CompilerParams(vmem_limit_bytes=24 * 2**20),
        name="finish",
    )(own_two, got, *[pltpu.with_memory_space_constraint(a, pltpu.HBM) for a in arrays])


FORWARD = [(r, (r + 2) % ROWS) for r in range(ROWS)]
BACKWARD = [(r, (r - 2) % ROWS) for r in range(ROWS)]
SWAP = [(r, r ^ 1) for r in range(ROWS)]


def per_device(
    root_inverse, factor_one, pivot_one, pattern_one, factor_two, pivot_two, pattern_two
):
    row = lax.axis_index("row")
    place = jnp.stack([row >> 1, row & 1]).astype(jnp.int32)
    col = lax.axis_index("col")
    factor_one = jnp.swapaxes(factor_one, 1, 2)
    factor_two = jnp.swapaxes(factor_two, 2, 3)
    high, low, child_high, child_low = prepare(factor_one, factor_two)
    shard = lax.all_to_all(pack(root_inverse), "col", 0, 0, tiled=True)
    halves = [shard[:, :4], shard[:, 4:]]
    behind = [lax.ppermute(half, "row", FORWARD) for half in halves]
    ahead = [lax.ppermute(half, "row", BACKWARD) for half in halves]
    across = [lax.ppermute(behind[0], "row", FORWARD), lax.ppermute(ahead[1], "row", BACKWARD)]
    pieces = []
    for piece in [shard] + ahead + behind:
        pieces += [piece, lax.ppermute(piece, "row", SWAP)]
    band = early(place, pattern_one, pieces)
    *across, band = lax.optimization_barrier((*across, band))
    pieces = []
    for piece in across:
        pieces += [piece, lax.ppermute(piece, "row", SWAP)]
    message = select(place, pattern_one, pattern_two, high, low, band, pieces)
    got = lax.all_to_all(message, "col", 0, 0, tiled=True)
    own_two = lax.dynamic_index_in_dim(pattern_two, col, 1, keepdims=False)
    column_one, diagonal_one, column_two, diagonal_two = finish(
        own_two,
        got.reshape(COLS * MESSAGE, 128),
        (high, low, child_high, child_low, pivot_one, pivot_two),
    )
    return (
        jnp.swapaxes(column_one, 1, 2),
        diagonal_one,
        jnp.swapaxes(column_two, 2, 3),
        diagonal_two,
    )


def solution(mesh):
    placed = (
        P("row", "col"),
        P("row", None, None),
        P("row", None, None),
        P("row", None),
        P("row", "col", None, None),
        P("row", "col", None, None),
        P("row", None, None),
    )
    return jax.shard_map(
        per_device,
        mesh=mesh,
        in_specs=placed,
        out_specs=(
            P("row", None, None),
            P("row", None, None),
            P("row", "col", None, None),
            P("row", "col", None, None),
        ),
        check_vma=False,
    )
```

```python
import jax
import jax.numpy as jnp
from jax import lax
from jax.experimental import pallas as pl
from jax.experimental.pallas import tpu as pltpu
from jax.sharding import PartitionSpec as P

F32 = jnp.float32
BF16 = jnp.bfloat16
BLOCK = 64
WIDTH = 192
ONE = 16
TWO = 6
OWN = 3
COLS = 16
ROWS = 8
SLICE = 4
UNITS = [(k, m) for k in range(TWO) for m in range(k + 1)]
BAND = ONE * SLICE
CHILD_TOP = 3 * BAND
MESSAGE = 280
WIDE = TWO * BLOCK
VMEM = pl.BlockSpec(memory_space=pltpu.VMEM)
SMEM = pl.BlockSpec(memory_space=pltpu.SMEM)
ANY = pl.BlockSpec(memory_space=pl.ANY)
HBM = pl.BlockSpec(memory_space=pltpu.HBM)


def in_hbm(arrays):
    return [pltpu.with_memory_space_constraint(array, pltpu.HBM) for array in arrays]


def split(value):
    high = value.astype(BF16)
    low = (value - high.astype(F32)).astype(BF16)
    return high, low


def product(left, right, dims=((1,), (0,))):
    def one(a, b):
        return lax.dot_general(a, b, (dims, ((), ())), preferred_element_type=F32)

    (lh, ll), (rh, rl) = left, right
    return one(lh, rh) + (one(lh, rl) + one(ll, rh))


def pack_kernel(root_ref, out_ref, near, ready, sems):
    def copies(tile):
        lanes = slice(128 * tile, 128 * tile + 128)
        return (
            pltpu.make_async_copy(root_ref.at[:, lanes], near.at[tile], sems.at[tile]),
            pltpu.make_async_copy(ready.at[tile], out_ref.at[:, :, :, lanes], sems.at[2 + tile]),
        )

    for tile in range(2):
        copies(tile)[0].start()
    for tile in range(2):
        copies(tile)[0].wait()
        for place in range(COLS):
            for n in range(8):
                ready[tile, place, n] = near[tile, pl.ds(BLOCK * n + place, SLICE, stride=16), :]
        copies(tile)[1].start()
    for tile in range(2):
        copies(tile)[1].wait()


def pack(root):
    return pl.pallas_call(
        pack_kernel,
        out_shape=pltpu.HBM((COLS, 8, SLICE, 256), F32),
        in_specs=[HBM],
        out_specs=HBM,
        scratch_shapes=[
            pltpu.VMEM((2, 512, 128), F32),
            pltpu.VMEM((2, COLS, 8, SLICE, 128), F32),
            pltpu.SemaphoreType.DMA((4,)),
        ],
        name="pack",
    )(*in_hbm([root]))


def pick_lanes(one_ref, parent, pair, side):
    block = one_ref[parent, 2 * pair + side]
    lanes = pl.ds(pl.multiple_of(((block >> 1) & 1) << 7, 128), 128)
    return block >> 2, lanes, ((block & 1) ^ side) << 6


def source_of(place_ref, block):
    return (((block >> 4) - place_ref[0]) & 3), ((block >> 3) & 1) == place_ref[1]


ROWS_SHAPE = (2, ONE, SLICE, ONE * BLOCK)


def early_kernel(
    place_ref, one_ref, other_ref, own_ref, low_ref, high_ref, far_factor,
    mine_out, other_out, split_high, split_low, rows, factor_ref, sem,
):
    left_half = lax.broadcasted_iota(jnp.int32, (ONE, SLICE, 128), 2) < BLOCK
    factor_copy = pltpu.make_async_copy(far_factor, factor_ref, sem)
    factor_copy.start()
    patterns = [(one_ref, 0), (one_ref, 1), (other_ref, 0), (other_ref, 1)]

    def row_step(a, carry):
        for parent, (pattern, n) in enumerate(patterns):
            block = pattern[n, a]
            step, here = source_of(place_ref, block)
            high = (block >> 2) & 1

            @pl.when(here)
            def _():
                @pl.when(step == 0)
                def _():
                    rows[parent, a] = own_ref[:, block & 7]

                @pl.when((step == 3) & (high == 0))
                def _():
                    rows[parent, a] = low_ref[:, block & 3]

                @pl.when((step == 1) & (high == 1))
                def _():
                    rows[parent, a] = high_ref[:, block & 3]

        return carry

    lax.fori_loop(0, ONE, row_step, 0)
    for parent, (pattern, n) in enumerate(patterns):
        for pair in range(ONE // 2):
            halves = []
            for side in range(2):
                source, lanes, turn = pick_lanes(pattern, n, pair, side)
                halves.append(pltpu.roll(rows[parent, :, source, :, lanes], turn, 2))
            lanes = slice(pair * 128, pair * 128 + 128)
            out = (mine_out, other_out)[parent // 2]
            out[n, :, :, lanes] = jnp.where(left_half, halves[0], halves[1])
    factor_copy.wait()
    for parent in range(2):
        split_high[parent], split_low[parent] = split(factor_ref[parent])


def early(place, pattern_one, pattern_other, factor, pieces):
    band = jax.ShapeDtypeStruct(ROWS_SHAPE, F32)
    halves = jax.ShapeDtypeStruct(factor.shape, BF16)
    return pl.pallas_call(
        early_kernel,
        out_shape=(band, band, halves, halves),
        in_specs=[SMEM] * 3 + [VMEM] * 3 + [HBM],
        out_specs=(VMEM,) * 4,
        scratch_shapes=[
            pltpu.VMEM((4, ONE, COLS, SLICE, 256), F32),
            pltpu.VMEM(factor.shape, F32),
            pltpu.SemaphoreType.DMA,
        ],
        compiler_params=pltpu.CompilerParams(vmem_limit_bytes=20 * 2**20),
        cost_estimate=pl.CostEstimate(flops=0, bytes_accessed=12 * 2**20, transcendentals=0),
        name="early",
    )(place, pattern_one, pattern_other, *pieces, *in_hbm([factor]))


def late_kernel(place_ref, one_ref, band_ref, ahead_ref, behind_ref, low_ref, high_ref, out_ref):
    left_half = lax.broadcasted_iota(jnp.int32, (SLICE, 128), 1) < BLOCK
    out_ref[...] = band_ref[...]

    def row_step(a, carry):
        for parent in range(2):
            block = one_ref[parent, a]
            step, here = source_of(place_ref, block)
            high = (block >> 2) & 1

            def fill(piece):
                for pair in range(ONE // 2):
                    halves = []
                    for side in range(2):
                        source, lanes, turn = pick_lanes(one_ref, parent, pair, side)
                        halves.append(pltpu.roll(piece[source, block & 3, :, lanes], turn, 1))
                    lanes = slice(pair * 128, pair * 128 + 128)
                    out_ref[parent, a, :, lanes] = jnp.where(left_half, halves[0], halves[1])

            @pl.when(here & (step != 0))
            def _():
                for place, half, piece in (
                    (1, 0, ahead_ref),
                    (3, 1, behind_ref),
                    (2, 0, low_ref),
                    (2, 1, high_ref),
                ):

                    @pl.when((step == place) & (high == half))
                    def _():
                        fill(piece)

        return carry

    lax.fori_loop(0, ONE, row_step, 0)


def late(place, pattern, band, pieces):
    return pl.pallas_call(
        late_kernel,
        out_shape=jax.ShapeDtypeStruct(ROWS_SHAPE, F32),
        in_specs=[SMEM] * 2 + [VMEM] * 5,
        out_specs=VMEM,
        compiler_params=pltpu.CompilerParams(vmem_limit_bytes=20 * 2**20),
        cost_estimate=pl.CostEstimate(flops=0, bytes_accessed=3 * 2**20, transcendentals=0),
        name="late",
    )(place, pattern, band, *pieces)


def select_kernel(
    place_ref, one_ref, two_ref, high_ref, low_ref, mine_ref, other_ref, out_ref, band, ready, sems
):
    left_half = lax.broadcasted_iota(jnp.int32, (SLICE, 128), 1) < BLOCK

    for parent in range(2):
        for a in range(ONE):
            here = source_of(place_ref, one_ref[parent, a])[1]
            for pair in range(ONE // 2):
                lanes = slice(pair * 128, pair * 128 + 128)
                value = jnp.where(
                    here, mine_ref[parent, a, :, lanes], other_ref[parent, a, :, lanes]
                )
                band[0, parent, a, :, lanes] = value
                band[1, parent, a, :, lanes] = pltpu.roll(value, BLOCK, 1)
    columns = jnp.concatenate(
        [
            -product(
                split(band[0, parent].reshape(BAND, ONE * BLOCK)),
                (high_ref[parent], low_ref[parent]),
                ((1,), (1,)),
            )
            for parent in range(2)
        ],
        axis=1,
    )
    for child in range(COLS):
        for tile in range(3):
            ready[child, tile * BAND : tile * BAND + BAND, :] = columns[
                :, 128 * tile : 128 * tile + 128
            ]

    def send(n):
        children = slice(0, COLS) if n == 0 else slice(8 * (n - 1), 8 * n)
        part = slice(0, CHILD_TOP) if n == 0 else slice(CHILD_TOP, MESSAGE)
        return pltpu.make_async_copy(
            ready.at[children, part], out_ref.at[children, part], sems.at[n]
        )

    def child_step(child, carry):
        picks = [
            [jnp.maximum(two_ref[parent, child, n] - OWN, 0) for n in range(TWO)]
            for parent in range(2)
        ]
        for unit, (k, m) in enumerate(UNITS):
            halves = []
            for parent in range(2):
                row, block = picks[parent][k], picks[parent][m]
                lanes = pl.ds(pl.multiple_of((block >> 1) << 7, 128), 128)
                halves.append(band[(block & 1) ^ parent, parent, row, :, lanes])
            top = CHILD_TOP + unit * SLICE
            ready[child, top : top + SLICE, :] = jnp.where(left_half, halves[0], halves[1])
        return carry

    send(0).start()
    lax.fori_loop(0, 8, child_step, 0, unroll=2)
    send(1).start()
    lax.fori_loop(8, COLS, child_step, 0, unroll=2)
    send(2).start()
    for n in range(3):
        send(n).wait()


def select(place, pattern_one, pattern_two, high, low, mine, other):
    return pl.pallas_call(
        select_kernel,
        out_shape=pltpu.HBM((COLS, MESSAGE, 128), F32),
        in_specs=[SMEM] * 3 + [VMEM] * 4,
        out_specs=HBM,
        scratch_shapes=[
            pltpu.VMEM((2,) + ROWS_SHAPE, F32),
            pltpu.VMEM((COLS, MESSAGE, 128), F32),
            pltpu.SemaphoreType.DMA((3,)),
        ],
        compiler_params=pltpu.CompilerParams(vmem_limit_bytes=20 * 2**20),
        name="select",
    )(place, pattern_one, pattern_two, high, low, mine, other)


def final_kernel(two_ref, got_ref, *refs):
    (far_in, far_out, beside, chosen, near_in, near_out, sems) = (
        refs[:4], refs[4:8], refs[8:10], refs[10:12], refs[12:16], refs[16:20], refs[20],
    )
    factor_ref, child_factor_ref, pivot_ref, child_pivot_ref = near_in
    column_ref, diagonal_ref, child_column_ref, child_diagonal_ref = near_out
    fetches = [
        pltpu.make_async_copy(far, near, sems.at[n])
        for n, (far, near) in enumerate(zip(far_in, near_in))
    ]
    stores = [
        [
            pltpu.make_async_copy(near.at[parent], far.at[parent], sems.at[4 + 2 * n + parent])
            for parent in range(2)
        ]
        for n, (far, near) in enumerate(zip(far_out, near_out))
    ]
    for fetch in fetches:
        fetch.start()
    left_half = lax.broadcasted_iota(jnp.int32, (16, 128), 1) < BLOCK
    left_block = lax.broadcasted_iota(jnp.int32, (BLOCK, 128), 1) < BLOCK
    nt = ((1,), (1,))
    for n in range(BAND):
        tiles = [got_ref[pl.ds(m * BAND + n, 16, stride=MESSAGE), :] for m in range(3)]
        here = slice(WIDTH + 16 * n, WIDTH + 16 * n + 16)
        turned = [pltpu.roll(tile, BLOCK, 1) for tile in tiles[1:]]
        beside[0][here, 0:128] = tiles[0]
        beside[0][here, 128:256] = tiles[1]
        beside[1][here, 0:128] = jnp.where(left_half, turned[0], turned[1])
        beside[1][here, 128:256] = turned[1]
    for parent in range(2):
        column_ref[parent] = beside[parent][WIDTH:, 0:WIDTH].T
        stores[0][parent].start()
    fetches[0].wait()
    fetches[2].wait()
    for parent in range(2):
        diagonal = pivot_ref[parent] - product(
            split(factor_ref[parent]), split(beside[parent][WIDTH:, 0:WIDTH])
        )
        diagonal_ref[parent] = diagonal
        beside[parent][0:WIDTH, 0:WIDTH] = diagonal
        stores[1][parent].start()
    for unit, (k, m) in enumerate(UNITS):
        for n in range(SLICE):
            value = got_ref[pl.ds(CHILD_TOP + unit * SLICE + n, 16, stride=MESSAGE), :]
            turned = pltpu.roll(value, BLOCK, 1)
            here = slice(BLOCK * k + 16 * n, BLOCK * k + 16 * n + 16)
            lanes = slice(BLOCK * m, BLOCK * m + BLOCK)
            half = slice(0, BLOCK) if m % 2 == 0 else slice(BLOCK, 128)
            chosen[m % 2][here, lanes] = value[:, half]
            chosen[1 - m % 2][here, lanes] = turned[:, half]
    row_block = lax.broadcasted_iota(jnp.int32, (WIDE, WIDE), 0) // BLOCK
    lane_block = lax.broadcasted_iota(jnp.int32, (WIDE, WIDE), 1) // BLOCK
    for parent in range(2):
        picks = [two_ref[parent, n] for n in range(TWO)]
        for k in range(TWO):
            here = slice(BLOCK * k, BLOCK * k + BLOCK)
            rows = pl.ds(pl.multiple_of(picks[k] << 6, BLOCK), BLOCK)
            tiles = [beside[parent][rows, 128 * n : 128 * n + 128] for n in range(2)]
            turned = [pltpu.roll(tile, BLOCK, 1) for tile in tiles]
            even = jnp.where(
                picks[0] == 0, tiles[0], jnp.where(picks[0] == 1, turned[0], tiles[1])
            )
            odd = jnp.where(picks[1] == 1, tiles[0], turned[1])
            near = chosen[parent][here, 0:128]
            chosen[parent][here, 0:128] = jnp.where(
                left_block,
                jnp.where(picks[0] >= OWN, near, even),
                jnp.where(picks[1] >= OWN, near, odd),
            )
            if k >= 2:
                near = chosen[parent][here, 128:256]
                chosen[parent][here, 128:256] = jnp.where(
                    left_block & (picks[2] < OWN), tiles[1], near
                )
    fetches[1].wait()
    fetches[3].wait()
    factors = [split(child_factor_ref[parent, 0]) for parent in range(2)]
    results = []
    for parent in range(2):
        lower = chosen[parent][...]
        whole = jnp.where(row_block >= lane_block, lower, lower.T)
        results.append(-product(factors[parent], split(whole)))
    for parent in range(2):
        child_column_ref[parent, 0] = results[parent]
        stores[2][parent].start()
    for parent in range(2):
        child_diagonal_ref[parent, 0] = child_pivot_ref[parent, 0] - product(
            factors[parent], split(results[parent]), nt
        )
        stores[3][parent].start()
    for pair in stores:
        for store in pair:
            store.wait()


def finish(own_two, got, arrays):
    shapes = (
        (2, WIDTH, ONE * BLOCK),
        (2, WIDTH, WIDTH),
        (2, 1, WIDTH, WIDE),
        (2, 1, WIDTH, WIDTH),
    )
    return pl.pallas_call(
        final_kernel,
        out_shape=tuple(pltpu.HBM(shape, F32) for shape in shapes),
        in_specs=[SMEM, VMEM] + [HBM] * 4,
        out_specs=(HBM,) * 4,
        scratch_shapes=[pltpu.VMEM((WIDTH + ONE * BLOCK, 256), F32)] * 2
        + [pltpu.VMEM((WIDE, WIDE), F32)] * 2
        + [pltpu.VMEM(array.shape, array.dtype) for array in arrays]
        + [pltpu.VMEM(shape, F32) for shape in shapes]
        + [pltpu.SemaphoreType.DMA((12,))],
        compiler_params=pltpu.CompilerParams(vmem_limit_bytes=24 * 2**20),
        name="finish",
    )(own_two, got, *in_hbm(arrays))


FORWARD = [(r, (r + 2) % ROWS) for r in range(ROWS)]
BACKWARD = [(r, (r - 2) % ROWS) for r in range(ROWS)]
SWAP = [(r, r ^ 1) for r in range(ROWS)]


def per_device(
    root_inverse, factor_one, pivot_one, pattern_one, factor_two, pivot_two, pattern_two
):
    row = lax.axis_index("row")
    place = jnp.stack([row >> 1, row & 1]).astype(jnp.int32)
    col = lax.axis_index("col")
    pattern_other = lax.ppermute(pattern_one, "row", SWAP)
    factor_one = jnp.swapaxes(factor_one, 1, 2)
    factor_two = jnp.swapaxes(factor_two, 2, 3)
    shard = lax.all_to_all(pack(root_inverse), "col", 0, 0, tiled=True)
    shard, pattern_other = lax.optimization_barrier((shard, pattern_other))
    halves = [shard[:, :4], shard[:, 4:]]
    behind = [lax.ppermute(half, "row", FORWARD) for half in halves]
    ahead = [lax.ppermute(half, "row", BACKWARD) for half in halves]
    across = [lax.ppermute(behind[0], "row", FORWARD), lax.ppermute(ahead[1], "row", BACKWARD)]
    mine, other, high, low = early(
        place, pattern_one, pattern_other, factor_one, [shard, behind[0], ahead[1]]
    )
    across = [ahead[0], behind[1]] + across
    other = lax.ppermute(late(place, pattern_other, other, across), "row", SWAP)
    mine = late(place, pattern_one, mine, across)
    message = select(place, pattern_one, pattern_two, high, low, mine, other)
    got = lax.all_to_all(message, "col", 0, 0, tiled=True)
    own_two = lax.dynamic_index_in_dim(pattern_two, col, 1, keepdims=False)
    column_one, diagonal_one, column_two, diagonal_two = finish(
        own_two,
        got.reshape(COLS * MESSAGE, 128),
        (factor_one, factor_two, pivot_one, pivot_two),
    )
    return (
        jnp.swapaxes(column_one, 1, 2),
        diagonal_one,
        jnp.swapaxes(column_two, 2, 3),
        diagonal_two,
    )


def solution(mesh):
    placed = (
        P("row", "col"),
        P("row", None, None),
        P("row", None, None),
        P("row", None),
        P("row", "col", None, None),
        P("row", "col", None, None),
        P("row", None, None),
    )
    return jax.shard_map(
        per_device,
        mesh=mesh,
        in_specs=placed,
        out_specs=(
            P("row", None, None),
            P("row", None, None),
            P("row", "col", None, None),
            P("row", "col", None, None),
        ),
        check_vma=False,
    )
```

```python
import functools

import jax
import jax.numpy as jnp
from jax import lax
from jax.experimental import pallas as pl
from jax.experimental.pallas import tpu as pltpu
from jax.sharding import PartitionSpec as P

F32 = jnp.float32
BF16 = jnp.bfloat16
BLOCK = 64
WIDTH = 192
ONE = 16
TWO = 6
OWN = 3
COLS = 16
ROWS = 8
SLICE = 4
UNITS = [(k, m) for k in range(TWO) for m in range(k + 1)]
BAND = ONE * SLICE
CHILD_TOP = 3 * BAND
MESSAGE = 280
WIDE = TWO * BLOCK
VMEM = pl.BlockSpec(memory_space=pltpu.VMEM)
SMEM = pl.BlockSpec(memory_space=pltpu.SMEM)
ANY = pl.BlockSpec(memory_space=pl.ANY)
HBM = pl.BlockSpec(memory_space=pltpu.HBM)


def in_hbm(arrays):
    return [pltpu.with_memory_space_constraint(array, pltpu.HBM) for array in arrays]


def split(value):
    high = value.astype(BF16)
    low = (value - high.astype(F32)).astype(BF16)
    return high, low


def product(left, right, dims=((1,), (0,))):
    def one(a, b):
        return lax.dot_general(a, b, (dims, ((), ())), preferred_element_type=F32)

    (lh, ll), (rh, rl) = left, right
    return one(lh, rh) + (one(lh, rl) + one(ll, rh))


def pack_kernel(root_ref, out_ref, near, ready, sems):
    def fetch(n, tile):
        here, lanes = slice(BLOCK * n, BLOCK * n + BLOCK), slice(128 * tile, 128 * tile + 128)
        return pltpu.make_async_copy(
            root_ref.at[here, lanes], near.at[tile, here], sems.at[0, n, tile]
        )

    def store(n):
        return pltpu.make_async_copy(ready.at[n], out_ref.at[:, n], sems.at[1, n, 0])

    for n in range(8):
        for tile in range(2):
            fetch(n, tile).start()
    for n in range(8):
        for tile in range(2):
            fetch(n, tile).wait()
            for place in range(COLS):
                ready[n, place, :, 128 * tile : 128 * tile + 128] = near[
                    tile, pl.ds(BLOCK * n + place, SLICE, stride=16), :
                ]
        store(n).start()
    for n in range(8):
        store(n).wait()


def pack(root):
    return pl.pallas_call(
        pack_kernel,
        out_shape=pltpu.HBM((COLS, 8, SLICE, 256), F32),
        in_specs=[HBM],
        out_specs=HBM,
        scratch_shapes=[
            pltpu.VMEM((2, 512, 128), F32),
            pltpu.VMEM((8, COLS, SLICE, 256), F32),
            pltpu.SemaphoreType.DMA((2, 8, 2)),
        ],
        name="pack",
    )(*in_hbm([root]))


def pick_lanes(one_ref, parent, pair, side):
    block = one_ref[parent, 2 * pair + side]
    lanes = pl.ds(pl.multiple_of(((block >> 1) & 1) << 7, 128), 128)
    return block >> 2, lanes, ((block & 1) ^ side) << 6


def source_of(place_ref, block):
    return (((block >> 4) - place_ref[0]) & 3), ((block >> 3) & 1) == place_ref[1]


ROWS_SHAPE = (2, ONE, SLICE, ONE * BLOCK)


def early_kernel(
    place_ref, one_ref, other_ref, own_ref, low_ref, high_ref, far_factor,
    mine_out, other_out, split_high, split_low, rows, factor_ref, sem,
):
    left_half = lax.broadcasted_iota(jnp.int32, (ONE, SLICE, 128), 2) < BLOCK
    factor_copy = pltpu.make_async_copy(far_factor, factor_ref, sem)
    factor_copy.start()
    patterns = [(one_ref, 0), (one_ref, 1), (other_ref, 0), (other_ref, 1)]

    def row_step(a, carry):
        for parent, (pattern, n) in enumerate(patterns):
            block = pattern[n, a]
            step, here = source_of(place_ref, block)
            high = (block >> 2) & 1

            @pl.when(here)
            def _():
                @pl.when(step == 0)
                def _():
                    rows[parent, a] = own_ref[:, block & 7]

                @pl.when((step == 3) & (high == 0))
                def _():
                    rows[parent, a] = low_ref[:, block & 3]

                @pl.when((step == 1) & (high == 1))
                def _():
                    rows[parent, a] = high_ref[:, block & 3]

        return carry

    lax.fori_loop(0, ONE, row_step, 0)
    for parent, (pattern, n) in enumerate(patterns):
        for pair in range(ONE // 2):
            halves = []
            for side in range(2):
                source, lanes, turn = pick_lanes(pattern, n, pair, side)
                halves.append(pltpu.roll(rows[parent, :, source, :, lanes], turn, 2))
            lanes = slice(pair * 128, pair * 128 + 128)
            out = (mine_out, other_out)[parent // 2]
            out[n, :, :, lanes] = jnp.where(left_half, halves[0], halves[1])
    factor_copy.wait()
    for parent in range(2):
        split_high[parent], split_low[parent] = split(factor_ref[parent])


def early(place, pattern_one, pattern_other, factor, pieces):
    band = jax.ShapeDtypeStruct(ROWS_SHAPE, F32)
    halves = jax.ShapeDtypeStruct(factor.shape, BF16)
    return pl.pallas_call(
        early_kernel,
        out_shape=(band, band, halves, halves),
        in_specs=[SMEM] * 3 + [VMEM] * 3 + [HBM],
        out_specs=(VMEM,) * 4,
        scratch_shapes=[
            pltpu.VMEM((4, ONE, COLS, SLICE, 256), F32),
            pltpu.VMEM(factor.shape, F32),
            pltpu.SemaphoreType.DMA,
        ],
        compiler_params=pltpu.CompilerParams(vmem_limit_bytes=20 * 2**20),
        cost_estimate=pl.CostEstimate(flops=0, bytes_accessed=12 * 2**20, transcendentals=0),
        name="early",
    )(place, pattern_one, pattern_other, *pieces, *in_hbm([factor]))


def fill_kernel(whence, place_ref, *refs):
    count = (len(refs) - len(whence)) // 3
    patterns, bands, outs = refs[:count], refs[count : 2 * count], refs[-count:]
    pieces = refs[2 * count : -count]
    left_half = lax.broadcasted_iota(jnp.int32, (SLICE, 128), 1) < BLOCK
    for band, out in zip(bands, outs):
        out[...] = band[...]

    def row_step(a, carry):
        for pattern, out in zip(patterns, outs):
            for parent in range(2):
                block = pattern[parent, a]
                step, here = source_of(place_ref, block)
                high = (block >> 2) & 1

                def fill(piece):
                    for pair in range(ONE // 2):
                        halves = []
                        for side in range(2):
                            source, lanes, turn = pick_lanes(pattern, parent, pair, side)
                            halves.append(pltpu.roll(piece[source, block & 3, :, lanes], turn, 1))
                        lanes = slice(pair * 128, pair * 128 + 128)
                        out[parent, a, :, lanes] = jnp.where(left_half, halves[0], halves[1])

                for (place, half), piece in zip(whence, pieces):

                    @pl.when(here & (step == place) & (high == half))
                    def _():
                        fill(piece)

        return carry

    lax.fori_loop(0, ONE, row_step, 0)


def fill(name, whence, place, patterns, bands, pieces):
    count = len(bands)
    return pl.pallas_call(
        functools.partial(fill_kernel, whence),
        out_shape=(jax.ShapeDtypeStruct(ROWS_SHAPE, F32),) * count,
        in_specs=[SMEM] * (1 + count) + [VMEM] * (count + len(pieces)),
        out_specs=(VMEM,) * count,
        compiler_params=pltpu.CompilerParams(vmem_limit_bytes=20 * 2**20),
        cost_estimate=pl.CostEstimate(flops=0, bytes_accessed=3 * 2**20, transcendentals=0),
        name=name,
    )(place, *patterns, *bands, *pieces)


def select_kernel(
    place_ref, one_ref, two_ref, high_ref, low_ref, mine_ref, other_ref, out_ref, band, ready, sems
):
    left_half = lax.broadcasted_iota(jnp.int32, (SLICE, 128), 1) < BLOCK

    for parent in range(2):
        for a in range(ONE):
            here = source_of(place_ref, one_ref[parent, a])[1]
            for pair in range(ONE // 2):
                lanes = slice(pair * 128, pair * 128 + 128)
                value = jnp.where(
                    here, mine_ref[parent, a, :, lanes], other_ref[parent, a, :, lanes]
                )
                band[0, parent, a, :, lanes] = value
                band[1, parent, a, :, lanes] = pltpu.roll(value, BLOCK, 1)
    columns = jnp.concatenate(
        [
            -product(
                split(band[0, parent].reshape(BAND, ONE * BLOCK)),
                (high_ref[parent], low_ref[parent]),
                ((1,), (1,)),
            )
            for parent in range(2)
        ],
        axis=1,
    )
    for child in range(COLS):
        for tile in range(3):
            ready[child, tile * BAND : tile * BAND + BAND, :] = columns[
                :, 128 * tile : 128 * tile + 128
            ]

    def send(n):
        children = slice(0, COLS) if n == 0 else slice(8 * (n - 1), 8 * n)
        part = slice(0, CHILD_TOP) if n == 0 else slice(CHILD_TOP, MESSAGE)
        return pltpu.make_async_copy(
            ready.at[children, part], out_ref.at[children, part], sems.at[n]
        )

    def child_step(child, carry):
        picks = [
            [jnp.maximum(two_ref[parent, child, n] - OWN, 0) for n in range(TWO)]
            for parent in range(2)
        ]
        for unit, (k, m) in enumerate(UNITS):
            halves = []
            for parent in range(2):
                row, block = picks[parent][k], picks[parent][m]
                lanes = pl.ds(pl.multiple_of((block >> 1) << 7, 128), 128)
                halves.append(band[(block & 1) ^ parent, parent, row, :, lanes])
            top = CHILD_TOP + unit * SLICE
            ready[child, top : top + SLICE, :] = jnp.where(left_half, halves[0], halves[1])
        return carry

    send(0).start()
    lax.fori_loop(0, 8, child_step, 0, unroll=4)
    send(1).start()
    lax.fori_loop(8, COLS, child_step, 0, unroll=4)
    send(2).start()
    for n in range(3):
        send(n).wait()


def select(place, pattern_one, pattern_two, high, low, mine, other):
    return pl.pallas_call(
        select_kernel,
        out_shape=pltpu.HBM((COLS, MESSAGE, 128), F32),
        in_specs=[SMEM] * 3 + [VMEM] * 4,
        out_specs=HBM,
        scratch_shapes=[
            pltpu.VMEM((2,) + ROWS_SHAPE, F32),
            pltpu.VMEM((COLS, MESSAGE, 128), F32),
            pltpu.SemaphoreType.DMA((3,)),
        ],
        compiler_params=pltpu.CompilerParams(vmem_limit_bytes=20 * 2**20),
        name="select",
    )(place, pattern_one, pattern_two, high, low, mine, other)


def final_kernel(two_ref, got_ref, *refs):
    (far_in, far_out, beside, chosen, near_in, near_out, sems) = (
        refs[:4], refs[4:8], refs[8:10], refs[10:12], refs[12:16], refs[16:20], refs[20],
    )
    factor_ref, child_factor_ref, pivot_ref, child_pivot_ref = near_in
    column_ref, diagonal_ref, child_column_ref, child_diagonal_ref = near_out
    fetches = [
        pltpu.make_async_copy(far, near, sems.at[n])
        for n, (far, near) in enumerate(zip(far_in, near_in))
    ]
    stores = [
        [
            pltpu.make_async_copy(near.at[parent], far.at[parent], sems.at[4 + 2 * n + parent])
            for parent in range(2)
        ]
        for n, (far, near) in enumerate(zip(far_out, near_out))
    ]
    for fetch in fetches:
        fetch.start()
    left_half = lax.broadcasted_iota(jnp.int32, (16, 128), 1) < BLOCK
    left_block = lax.broadcasted_iota(jnp.int32, (BLOCK, 128), 1) < BLOCK
    nt = ((1,), (1,))
    for n in range(BAND):
        tiles = [got_ref[pl.ds(m * BAND + n, 16, stride=MESSAGE), :] for m in range(3)]
        here = slice(WIDTH + 16 * n, WIDTH + 16 * n + 16)
        turned = [pltpu.roll(tile, BLOCK, 1) for tile in tiles[1:]]
        beside[0][here, 0:128] = tiles[0]
        beside[0][here, 128:256] = tiles[1]
        beside[1][here, 0:128] = jnp.where(left_half, turned[0], turned[1])
        beside[1][here, 128:256] = turned[1]
    for parent in range(2):
        column_ref[parent] = beside[parent][WIDTH:, 0:WIDTH].T
        stores[0][parent].start()
    for unit, (k, m) in enumerate(UNITS):
        for n in range(SLICE):
            value = got_ref[pl.ds(CHILD_TOP + unit * SLICE + n, 16, stride=MESSAGE), :]
            turned = pltpu.roll(value, BLOCK, 1)
            here = slice(BLOCK * k + 16 * n, BLOCK * k + 16 * n + 16)
            lanes = slice(BLOCK * m, BLOCK * m + BLOCK)
            half = slice(0, BLOCK) if m % 2 == 0 else slice(BLOCK, 128)
            chosen[m % 2][here, lanes] = value[:, half]
            chosen[1 - m % 2][here, lanes] = turned[:, half]
    fetches[0].wait()
    fetches[2].wait()
    diagonals = [
        pivot_ref[parent]
        - product(split(factor_ref[parent]), split(beside[parent][WIDTH:, 0:WIDTH]))
        for parent in range(2)
    ]
    for parent in range(2):
        diagonal_ref[parent] = diagonals[parent]
        beside[parent][0:WIDTH, 0:WIDTH] = diagonals[parent]
    for parent in range(2):
        stores[1][parent].start()
    row_block = lax.broadcasted_iota(jnp.int32, (WIDE, WIDE), 0) // BLOCK
    lane_block = lax.broadcasted_iota(jnp.int32, (WIDE, WIDE), 1) // BLOCK
    for parent in range(2):
        picks = [two_ref[parent, n] for n in range(TWO)]
        for k in range(TWO):
            here = slice(BLOCK * k, BLOCK * k + BLOCK)
            rows = pl.ds(pl.multiple_of(picks[k] << 6, BLOCK), BLOCK)
            tiles = [beside[parent][rows, 128 * n : 128 * n + 128] for n in range(2)]
            turned = [pltpu.roll(tile, BLOCK, 1) for tile in tiles]
            even = jnp.where(
                picks[0] == 0, tiles[0], jnp.where(picks[0] == 1, turned[0], tiles[1])
            )
            odd = jnp.where(picks[1] == 1, tiles[0], turned[1])
            near = chosen[parent][here, 0:128]
            chosen[parent][here, 0:128] = jnp.where(
                left_block,
                jnp.where(picks[0] >= OWN, near, even),
                jnp.where(picks[1] >= OWN, near, odd),
            )
            if k >= 2:
                near = chosen[parent][here, 128:256]
                chosen[parent][here, 128:256] = jnp.where(
                    left_block & (picks[2] < OWN), tiles[1], near
                )
    fetches[1].wait()
    fetches[3].wait()
    factors = [split(child_factor_ref[parent, 0]) for parent in range(2)]
    results = []
    for parent in range(2):
        lower = chosen[parent][...]
        whole = jnp.where(row_block >= lane_block, lower, lower.T)
        results.append(-product(factors[parent], split(whole)))
    for parent in range(2):
        child_column_ref[parent, 0] = results[parent]
    for parent in range(2):
        stores[2][parent].start()
    diagonals = [
        child_pivot_ref[parent, 0] - product(factors[parent], split(results[parent]), nt)
        for parent in range(2)
    ]
    for parent in range(2):
        child_diagonal_ref[parent, 0] = diagonals[parent]
    for parent in range(2):
        stores[3][parent].start()
    for pair in stores:
        for store in pair:
            store.wait()


def finish(own_two, got, arrays):
    shapes = (
        (2, WIDTH, ONE * BLOCK),
        (2, WIDTH, WIDTH),
        (2, 1, WIDTH, WIDE),
        (2, 1, WIDTH, WIDTH),
    )
    return pl.pallas_call(
        final_kernel,
        out_shape=tuple(pltpu.HBM(shape, F32) for shape in shapes),
        in_specs=[SMEM, VMEM] + [HBM] * 4,
        out_specs=(HBM,) * 4,
        scratch_shapes=[pltpu.VMEM((WIDTH + ONE * BLOCK, 256), F32)] * 2
        + [pltpu.VMEM((WIDE, WIDE), F32)] * 2
        + [pltpu.VMEM(array.shape, array.dtype) for array in arrays]
        + [pltpu.VMEM(shape, F32) for shape in shapes]
        + [pltpu.SemaphoreType.DMA((12,))],
        compiler_params=pltpu.CompilerParams(vmem_limit_bytes=24 * 2**20),
        name="finish",
    )(own_two, got, *in_hbm(arrays))


FORWARD = [(r, (r + 2) % ROWS) for r in range(ROWS)]
BACKWARD = [(r, (r - 2) % ROWS) for r in range(ROWS)]
SWAP = [(r, r ^ 1) for r in range(ROWS)]


def per_device(
    root_inverse, factor_one, pivot_one, pattern_one, factor_two, pivot_two, pattern_two
):
    row = lax.axis_index("row")
    place = jnp.stack([row >> 1, row & 1]).astype(jnp.int32)
    col = lax.axis_index("col")
    pattern_other = lax.ppermute(pattern_one, "row", SWAP)
    factor_one = jnp.swapaxes(factor_one, 1, 2)
    factor_two = jnp.swapaxes(factor_two, 2, 3)
    shard = lax.all_to_all(pack(root_inverse), "col", 0, 0, tiled=True)
    shard, pattern_other = lax.optimization_barrier((shard, pattern_other))
    halves = [shard[:, :4], shard[:, 4:]]
    behind = [lax.ppermute(half, "row", FORWARD) for half in halves]
    ahead = [lax.ppermute(half, "row", BACKWARD) for half in halves]
    across = [lax.ppermute(behind[0], "row", FORWARD), lax.ppermute(ahead[1], "row", BACKWARD)]
    mine, other, high, low = early(
        place, pattern_one, pattern_other, factor_one, [shard, behind[0], ahead[1]]
    )
    mine, other = fill(
        "second",
        ((1, 0), (3, 1)),
        place,
        (pattern_one, pattern_other),
        (mine, other),
        (ahead[0], behind[1]),
    )
    relayed = ((2, 0), (2, 1))
    (other,) = fill("last", relayed, place, (pattern_other,), (other,), across)
    other = lax.ppermute(other, "row", SWAP)
    (mine,) = fill("last", relayed, place, (pattern_one,), (mine,), across)
    message = select(place, pattern_one, pattern_two, high, low, mine, other)
    got = lax.all_to_all(message, "col", 0, 0, tiled=True)
    own_two = lax.dynamic_index_in_dim(pattern_two, col, 1, keepdims=False)
    column_one, diagonal_one, column_two, diagonal_two = finish(
        own_two,
        got.reshape(COLS * MESSAGE, 128),
        (factor_one, factor_two, pivot_one, pivot_two),
    )
    return (
        jnp.swapaxes(column_one, 1, 2),
        diagonal_one,
        jnp.swapaxes(column_two, 2, 3),
        diagonal_two,
    )


def solution(mesh):
    placed = (
        P("row", "col"),
        P("row", None, None),
        P("row", None, None),
        P("row", None),
        P("row", "col", None, None),
        P("row", "col", None, None),
        P("row", None, None),
    )
    return jax.shard_map(
        per_device,
        mesh=mesh,
        in_specs=placed,
        out_specs=(
            P("row", None, None),
            P("row", None, None),
            P("row", "col", None, None),
            P("row", "col", None, None),
        ),
        check_vma=False,
    )
```

```python
import functools

import jax
import jax.numpy as jnp
from jax import lax
from jax.experimental import pallas as pl
from jax.experimental.pallas import tpu as pltpu
from jax.sharding import PartitionSpec as P

F32 = jnp.float32
BF16 = jnp.bfloat16
BLOCK = 64
WIDTH = 192
ONE = 16
TWO = 6
OWN = 3
COLS = 16
ROWS = 8
SLICE = 4
UNITS = [(k, m) for k in range(TWO) for m in range(k + 1)]
BAND = ONE * SLICE
CHILD_TOP = 3 * BAND
MESSAGE = 280
WIDE = TWO * BLOCK
VMEM = pl.BlockSpec(memory_space=pltpu.VMEM)
SMEM = pl.BlockSpec(memory_space=pltpu.SMEM)
ANY = pl.BlockSpec(memory_space=pl.ANY)
HBM = pl.BlockSpec(memory_space=pltpu.HBM)


def in_hbm(arrays):
    return [pltpu.with_memory_space_constraint(array, pltpu.HBM) for array in arrays]


def split(value):
    high = value.astype(BF16)
    low = (value - high.astype(F32)).astype(BF16)
    return high, low


def product(left, right, dims=((1,), (0,))):
    def one(a, b):
        return lax.dot_general(a, b, (dims, ((), ())), preferred_element_type=F32)

    (lh, ll), (rh, rl) = left, right
    return one(lh, rh) + (one(lh, rl) + one(ll, rh))


def pack_kernel(root_ref, out_ref, near, ready, sems):
    def fetch(n, tile):
        here, lanes = slice(BLOCK * n, BLOCK * n + BLOCK), slice(128 * tile, 128 * tile + 128)
        return pltpu.make_async_copy(
            root_ref.at[here, lanes], near.at[tile, here], sems.at[0, n, tile]
        )

    def store(n):
        return pltpu.make_async_copy(ready.at[n], out_ref.at[:, n], sems.at[1, n, 0])

    for n in range(8):
        for tile in range(2):
            fetch(n, tile).start()
    for n in range(8):
        for tile in range(2):
            fetch(n, tile).wait()
            for place in range(COLS):
                ready[n, place, :, 128 * tile : 128 * tile + 128] = near[
                    tile, pl.ds(BLOCK * n + place, SLICE, stride=16), :
                ]
        store(n).start()
    for n in range(8):
        store(n).wait()


def pack(root):
    return pl.pallas_call(
        pack_kernel,
        out_shape=pltpu.HBM((COLS, 8, SLICE, 256), F32),
        in_specs=[HBM],
        out_specs=HBM,
        scratch_shapes=[
            pltpu.VMEM((2, 512, 128), F32),
            pltpu.VMEM((8, COLS, SLICE, 256), F32),
            pltpu.SemaphoreType.DMA((2, 8, 2)),
        ],
        name="pack",
    )(*in_hbm([root]))


def pick_lanes(one_ref, parent, pair, side):
    block = one_ref[parent, 2 * pair + side]
    lanes = pl.ds(pl.multiple_of(((block >> 1) & 1) << 7, 128), 128)
    return block >> 2, lanes, ((block & 1) ^ side) << 6


def source_of(place_ref, block):
    return (((block >> 4) - place_ref[0]) & 3), ((block >> 3) & 1) == place_ref[1]


ROWS_SHAPE = (2, ONE, SLICE, ONE * BLOCK)


def early_kernel(
    place_ref, one_ref, other_ref, own_ref, low_ref, high_ref, far_factor,
    mine_out, other_out, split_high, split_low, rows, factor_ref, sem,
):
    left_half = lax.broadcasted_iota(jnp.int32, (ONE, SLICE, 128), 2) < BLOCK
    factor_copy = pltpu.make_async_copy(far_factor, factor_ref, sem)
    factor_copy.start()
    patterns = [(one_ref, 0), (one_ref, 1), (other_ref, 0), (other_ref, 1)]

    def row_step(a, carry):
        for parent, (pattern, n) in enumerate(patterns):
            block = pattern[n, a]
            step, here = source_of(place_ref, block)
            high = (block >> 2) & 1

            @pl.when(here)
            def _():
                @pl.when(step == 0)
                def _():
                    rows[parent, a] = own_ref[:, block & 7]

                @pl.when((step == 3) & (high == 0))
                def _():
                    rows[parent, a] = low_ref[:, block & 3]

                @pl.when((step == 1) & (high == 1))
                def _():
                    rows[parent, a] = high_ref[:, block & 3]

        return carry

    lax.fori_loop(0, ONE, row_step, 0)
    for parent, (pattern, n) in enumerate(patterns):
        for pair in range(ONE // 2):
            halves = []
            for side in range(2):
                source, lanes, turn = pick_lanes(pattern, n, pair, side)
                halves.append(pltpu.roll(rows[parent, :, source, :, lanes], turn, 2))
            lanes = slice(pair * 128, pair * 128 + 128)
            out = (mine_out, other_out)[parent // 2]
            out[n, :, :, lanes] = jnp.where(left_half, halves[0], halves[1])
    factor_copy.wait()
    for parent in range(2):
        split_high[parent], split_low[parent] = split(factor_ref[parent])


def early(place, pattern_one, pattern_other, factor, pieces):
    band = jax.ShapeDtypeStruct(ROWS_SHAPE, F32)
    halves = jax.ShapeDtypeStruct(factor.shape, BF16)
    return pl.pallas_call(
        early_kernel,
        out_shape=(band, band, halves, halves),
        in_specs=[SMEM] * 3 + [VMEM] * 3 + [HBM],
        out_specs=(VMEM,) * 4,
        scratch_shapes=[
            pltpu.VMEM((4, ONE, COLS, SLICE, 256), F32),
            pltpu.VMEM(factor.shape, F32),
            pltpu.SemaphoreType.DMA,
        ],
        compiler_params=pltpu.CompilerParams(vmem_limit_bytes=20 * 2**20),
        cost_estimate=pl.CostEstimate(flops=0, bytes_accessed=12 * 2**20, transcendentals=0),
        name="early",
    )(place, pattern_one, pattern_other, *pieces, *in_hbm([factor]))


def fill_kernel(whence, place_ref, *refs):
    count = (len(refs) - len(whence)) // 3
    patterns, bands, outs = refs[:count], refs[count : 2 * count], refs[-count:]
    pieces = refs[2 * count : -count]
    left_half = lax.broadcasted_iota(jnp.int32, (SLICE, 128), 1) < BLOCK
    for band, out in zip(bands, outs):
        out[...] = band[...]

    def row_step(a, carry):
        for pattern, out in zip(patterns, outs):
            for parent in range(2):
                block = pattern[parent, a]
                step, here = source_of(place_ref, block)
                high = (block >> 2) & 1

                def fill(piece):
                    for pair in range(ONE // 2):
                        halves = []
                        for side in range(2):
                            source, lanes, turn = pick_lanes(pattern, parent, pair, side)
                            halves.append(pltpu.roll(piece[source, block & 3, :, lanes], turn, 1))
                        lanes = slice(pair * 128, pair * 128 + 128)
                        out[parent, a, :, lanes] = jnp.where(left_half, halves[0], halves[1])

                @pl.when(here)
                def _():
                    for (place, half), piece in zip(whence, pieces):

                        @pl.when((step == place) & (high == half))
                        def _():
                            fill(piece)

        return carry

    lax.fori_loop(0, ONE, row_step, 0)


def fill(name, whence, place, patterns, bands, pieces):
    count = len(bands)
    return pl.pallas_call(
        functools.partial(fill_kernel, whence),
        out_shape=(jax.ShapeDtypeStruct(ROWS_SHAPE, F32),) * count,
        in_specs=[SMEM] * (1 + count) + [VMEM] * (count + len(pieces)),
        out_specs=(VMEM,) * count,
        compiler_params=pltpu.CompilerParams(vmem_limit_bytes=20 * 2**20),
        cost_estimate=pl.CostEstimate(flops=0, bytes_accessed=3 * 2**20, transcendentals=0),
        name=name,
    )(place, *patterns, *bands, *pieces)


def select_kernel(
    place_ref, one_ref, two_ref, high_ref, low_ref, mine_ref, other_ref, out_ref, band, ready, sems
):
    left_half = lax.broadcasted_iota(jnp.int32, (SLICE, 128), 1) < BLOCK

    for parent in range(2):
        for a in range(ONE):
            here = source_of(place_ref, one_ref[parent, a])[1]
            for tile in range(ONE // 2):
                lanes = slice(tile * 128, tile * 128 + 128)
                value = jnp.where(
                    here, mine_ref[parent, a, :, lanes], other_ref[parent, a, :, lanes]
                )
                at = (parent * 8 + tile) * ONE + a
                band[at] = value
                band[256 + at] = pltpu.roll(value, BLOCK, 1)

    def rows_of(parent):
        tiles = [
            band[(parent * 8 + tile) * ONE : (parent * 8 + tile + 1) * ONE].reshape(BAND, 128)
            for tile in range(ONE // 2)
        ]
        return jnp.concatenate(tiles, axis=1)

    columns = jnp.concatenate(
        [
            -product(
                split(rows_of(parent)), (high_ref[parent], low_ref[parent]), ((1,), (1,))
            )
            for parent in range(2)
        ],
        axis=1,
    )
    for child in range(COLS):
        for tile in range(3):
            ready[child, tile * BAND : tile * BAND + BAND, :] = columns[
                :, 128 * tile : 128 * tile + 128
            ]

    def send(n):
        children = slice(0, COLS) if n == 0 else slice(8 * (n - 1), 8 * n)
        part = slice(0, CHILD_TOP) if n == 0 else slice(CHILD_TOP, MESSAGE)
        return pltpu.make_async_copy(
            ready.at[children, part], out_ref.at[children, part], sems.at[n]
        )

    def child_step(child, carry):
        picks = [
            [jnp.maximum(two_ref[parent, child, n] - OWN, 0) for n in range(TWO)]
            for parent in range(2)
        ]
        places = [
            [
                256 * ((block & 1) ^ parent) + 128 * parent + ((block >> 1) << 4)
                for block in picks[parent]
            ]
            for parent in range(2)
        ]
        for unit, (k, m) in enumerate(UNITS):
            halves = [band[picks[parent][k] + places[parent][m]] for parent in range(2)]
            top = CHILD_TOP + unit * SLICE
            ready[child, top : top + SLICE, :] = jnp.where(left_half, halves[0], halves[1])
        return carry

    send(0).start()
    lax.fori_loop(0, 8, child_step, 0, unroll=4)
    send(1).start()
    lax.fori_loop(8, COLS, child_step, 0, unroll=4)
    send(2).start()
    for n in range(3):
        send(n).wait()


def select(place, pattern_one, pattern_two, high, low, mine, other):
    return pl.pallas_call(
        select_kernel,
        out_shape=pltpu.HBM((COLS, MESSAGE, 128), F32),
        in_specs=[SMEM] * 3 + [VMEM] * 4,
        out_specs=HBM,
        scratch_shapes=[
            pltpu.VMEM((512, SLICE, 128), F32),
            pltpu.VMEM((COLS, MESSAGE, 128), F32),
            pltpu.SemaphoreType.DMA((3,)),
        ],
        compiler_params=pltpu.CompilerParams(vmem_limit_bytes=20 * 2**20),
        name="select",
    )(place, pattern_one, pattern_two, high, low, mine, other)


def final_kernel(place_ref, two_ref, got_ref, *refs):
    (far_in, far_out, beside, chosen, near_in, near_out, sems) = (
        refs[:4], refs[4:8], refs[8:10], refs[10:12], refs[12:16], refs[16:20], refs[20],
    )
    factor_ref, _, _, child_pivot_ref = near_in
    child_factor_ref, pivot_ref = far_in[1:3]
    column_ref, diagonal_ref, child_column_ref, child_diagonal_ref = near_out
    fetches = [
        pltpu.make_async_copy(far, near, sems.at[n])
        for n, (far, near) in enumerate(zip(far_in, near_in))
    ]
    stores = [
        [
            pltpu.make_async_copy(near.at[parent], far.at[parent], sems.at[4 + 2 * n + parent])
            for parent in range(2)
        ]
        for n, (far, near) in enumerate(zip(far_out, near_out))
    ]
    fetches[0].start()
    left_half = lax.broadcasted_iota(jnp.int32, (16, 128), 1) < BLOCK
    left_block = lax.broadcasted_iota(jnp.int32, (BLOCK, 128), 1) < BLOCK
    nt = ((1,), (1,))
    for n in range(BAND):
        tiles = [got_ref[pl.ds(m * BAND + n, 16, stride=MESSAGE), :] for m in range(3)]
        here = slice(WIDTH + 16 * n, WIDTH + 16 * n + 16)
        turned = [pltpu.roll(tile, BLOCK, 1) for tile in tiles[1:]]
        beside[0][here, 0:128] = tiles[0]
        beside[0][here, 128:256] = tiles[1]
        beside[1][here, 0:128] = jnp.where(left_half, turned[0], turned[1])
        beside[1][here, 128:256] = turned[1]
    fetches[3].start()
    for parent in range(2):
        column_ref[parent] = beside[parent][WIDTH:, 0:WIDTH].T
        stores[0][parent].start()
    for unit, (k, m) in enumerate(UNITS):
        for n in range(SLICE):
            value = got_ref[pl.ds(CHILD_TOP + unit * SLICE + n, 16, stride=MESSAGE), :]
            turned = pltpu.roll(value, BLOCK, 1)
            here = slice(BLOCK * k + 16 * n, BLOCK * k + 16 * n + 16)
            lanes = slice(BLOCK * m, BLOCK * m + BLOCK)
            half = slice(0, BLOCK) if m % 2 == 0 else slice(BLOCK, 128)
            chosen[m % 2][here, lanes] = value[:, half]
            chosen[1 - m % 2][here, lanes] = turned[:, half]
    fetches[0].wait()
    diagonals = [
        pivot_ref[parent]
        - product(split(factor_ref[parent]), split(beside[parent][WIDTH:, 0:WIDTH]))
        for parent in range(2)
    ]
    for parent in range(2):
        diagonal_ref[parent] = diagonals[parent]
        beside[parent][0:WIDTH, 0:WIDTH] = diagonals[parent]
    for parent in range(2):
        stores[1][parent].start()
    row_block = lax.broadcasted_iota(jnp.int32, (WIDE, WIDE), 0) // BLOCK
    lane_block = lax.broadcasted_iota(jnp.int32, (WIDE, WIDE), 1) // BLOCK
    for parent in range(2):
        picks = [two_ref[parent, place_ref[2], n] for n in range(TWO)]
        for k in range(TWO):
            here = slice(BLOCK * k, BLOCK * k + BLOCK)
            rows = pl.ds(pl.multiple_of(picks[k] << 6, BLOCK), BLOCK)
            tiles = [beside[parent][rows, 128 * n : 128 * n + 128] for n in range(2)]
            turned = [pltpu.roll(tile, BLOCK, 1) for tile in tiles]
            even = jnp.where(
                picks[0] == 0, tiles[0], jnp.where(picks[0] == 1, turned[0], tiles[1])
            )
            odd = jnp.where(picks[1] == 1, tiles[0], turned[1])
            near = chosen[parent][here, 0:128]
            chosen[parent][here, 0:128] = jnp.where(
                left_block,
                jnp.where(picks[0] >= OWN, near, even),
                jnp.where(picks[1] >= OWN, near, odd),
            )
            if k >= 2:
                near = chosen[parent][here, 128:256]
                chosen[parent][here, 128:256] = jnp.where(
                    left_block & (picks[2] < OWN), tiles[1], near
                )
    fetches[3].wait()
    factors = [split(child_factor_ref[parent, 0]) for parent in range(2)]
    results = []
    for parent in range(2):
        lower = chosen[parent][...]
        whole = jnp.where(row_block >= lane_block, lower, lower.T)
        results.append(-product(factors[parent], split(whole)))
    for parent in range(2):
        child_column_ref[parent, 0] = results[parent]
    for parent in range(2):
        stores[2][parent].start()
    diagonals = [
        child_pivot_ref[parent, 0] - product(factors[parent], split(results[parent]), nt)
        for parent in range(2)
    ]
    for parent in range(2):
        child_diagonal_ref[parent, 0] = diagonals[parent]
    for parent in range(2):
        stores[3][parent].start()
    for pair in stores:
        for store in pair:
            store.wait()


def finish(place, pattern_two, got, arrays):
    shapes = (
        (2, WIDTH, ONE * BLOCK),
        (2, WIDTH, WIDTH),
        (2, 1, WIDTH, WIDE),
        (2, 1, WIDTH, WIDTH),
    )
    return pl.pallas_call(
        final_kernel,
        out_shape=tuple(pltpu.HBM(shape, F32) for shape in shapes),
        in_specs=[SMEM, SMEM, VMEM] + [HBM, VMEM, VMEM, HBM],
        out_specs=(HBM,) * 4,
        scratch_shapes=[pltpu.VMEM((WIDTH + ONE * BLOCK, 256), F32)] * 2
        + [pltpu.VMEM((WIDE, WIDE), F32)] * 2
        + [pltpu.VMEM(array.shape, array.dtype) for array in arrays]
        + [pltpu.VMEM(shape, F32) for shape in shapes]
        + [pltpu.SemaphoreType.DMA((12,))],
        compiler_params=pltpu.CompilerParams(vmem_limit_bytes=24 * 2**20),
        name="finish",
    )(place, pattern_two, got, *in_hbm(arrays[:1]), *arrays[1:3], *in_hbm(arrays[3:]))


FORWARD = [(r, (r + 2) % ROWS) for r in range(ROWS)]
BACKWARD = [(r, (r - 2) % ROWS) for r in range(ROWS)]
SWAP = [(r, r ^ 1) for r in range(ROWS)]


def per_device(
    root_inverse, factor_one, pivot_one, pattern_one, factor_two, pivot_two, pattern_two
):
    row = lax.axis_index("row")
    col = lax.axis_index("col")
    place = jnp.stack([row >> 1, row & 1, col]).astype(jnp.int32)
    pattern_other = lax.ppermute(pattern_one, "row", SWAP)
    factor_one = jnp.swapaxes(factor_one, 1, 2)
    factor_two = jnp.swapaxes(factor_two, 2, 3)
    shard = lax.all_to_all(pack(root_inverse), "col", 0, 0, tiled=True)
    shard, pattern_other = lax.optimization_barrier((shard, pattern_other))
    halves = [shard[:, :4], shard[:, 4:]]
    behind = [lax.ppermute(half, "row", FORWARD) for half in halves]
    ahead = [lax.ppermute(half, "row", BACKWARD) for half in halves]
    across = [lax.ppermute(behind[0], "row", FORWARD), lax.ppermute(ahead[1], "row", BACKWARD)]
    mine, other, high, low = early(
        place, pattern_one, pattern_other, factor_one, [shard, behind[0], ahead[1]]
    )
    mine, other = fill(
        "second",
        ((1, 0), (3, 1)),
        place,
        (pattern_one, pattern_other),
        (mine, other),
        (ahead[0], behind[1]),
    )
    relayed = ((2, 0), (2, 1))
    (other,) = fill("last", relayed, place, (pattern_other,), (other,), across)
    other = lax.ppermute(other, "row", SWAP)
    (mine,) = fill("last", relayed, place, (pattern_one,), (mine,), across)
    message = select(place, pattern_one, pattern_two, high, low, mine, other)
    got = lax.all_to_all(message, "col", 0, 0, tiled=True)
    column_one, diagonal_one, column_two, diagonal_two = finish(
        place,
        pattern_two,
        got.reshape(COLS * MESSAGE, 128),
        (factor_one, factor_two, pivot_one, pivot_two),
    )
    return (
        jnp.swapaxes(column_one, 1, 2),
        diagonal_one,
        jnp.swapaxes(column_two, 2, 3),
        diagonal_two,
    )


def solution(mesh):
    placed = (
        P("row", "col"),
        P("row", None, None),
        P("row", None, None),
        P("row", None),
        P("row", "col", None, None),
        P("row", "col", None, None),
        P("row", None, None),
    )
    return jax.shard_map(
        per_device,
        mesh=mesh,
        in_specs=placed,
        out_specs=(
            P("row", None, None),
            P("row", None, None),
            P("row", "col", None, None),
            P("row", "col", None, None),
        ),
        check_vma=False,
    )
```

```python
import functools

import jax
import jax.numpy as jnp
from jax import lax
from jax.experimental import pallas as pl
from jax.experimental.pallas import tpu as pltpu
from jax.sharding import PartitionSpec as P

F32 = jnp.float32
BF16 = jnp.bfloat16
BLOCK = 64
WIDTH = 192
ONE = 16
TWO = 6
OWN = 3
COLS = 16
ROWS = 8
SLICE = 4
UNITS = [(k, m) for k in range(TWO) for m in range(k + 1)]
BAND = ONE * SLICE
CHILD_TOP = 3 * BAND
MESSAGE = 280
WIDE = TWO * BLOCK
VMEM = pl.BlockSpec(memory_space=pltpu.VMEM)
SMEM = pl.BlockSpec(memory_space=pltpu.SMEM)
ANY = pl.BlockSpec(memory_space=pl.ANY)
HBM = pl.BlockSpec(memory_space=pltpu.HBM)


def in_hbm(arrays):
    return [pltpu.with_memory_space_constraint(array, pltpu.HBM) for array in arrays]


def split(value):
    high = value.astype(BF16)
    low = (value - high.astype(F32)).astype(BF16)
    return high, low


def product(left, right, dims=((1,), (0,))):
    def one(a, b):
        return lax.dot_general(a, b, (dims, ((), ())), preferred_element_type=F32)

    (lh, ll), (rh, rl) = left, right
    return one(lh, rh) + (one(lh, rl) + one(ll, rh))


def pack_kernel(root_ref, out_ref, near, ready, sems):
    def fetch(n, tile):
        here, lanes = slice(BLOCK * n, BLOCK * n + BLOCK), slice(128 * tile, 128 * tile + 128)
        return pltpu.make_async_copy(
            root_ref.at[here, lanes], near.at[tile, here], sems.at[0, n, tile]
        )

    def store(n):
        return pltpu.make_async_copy(ready.at[n], out_ref.at[:, n], sems.at[1, n, 0])

    for n in range(8):
        for tile in range(2):
            fetch(n, tile).start()
    for n in range(8):
        for tile in range(2):
            fetch(n, tile).wait()
            for place in range(COLS):
                ready[n, place, :, 128 * tile : 128 * tile + 128] = near[
                    tile, pl.ds(BLOCK * n + place, SLICE, stride=16), :
                ]
        store(n).start()
    for n in range(8):
        store(n).wait()


def pack(root):
    return pl.pallas_call(
        pack_kernel,
        out_shape=pltpu.HBM((COLS, 8, SLICE, 256), F32),
        in_specs=[HBM],
        out_specs=HBM,
        scratch_shapes=[
            pltpu.VMEM((2, 512, 128), F32),
            pltpu.VMEM((8, COLS, SLICE, 256), F32),
            pltpu.SemaphoreType.DMA((2, 8, 2)),
        ],
        name="pack",
    )(*in_hbm([root]))


def pick_lanes(one_ref, parent, pair, side):
    block = one_ref[parent, 2 * pair + side]
    lanes = pl.ds(pl.multiple_of(((block >> 1) & 1) << 7, 128), 128)
    return block >> 2, lanes, ((block & 1) ^ side) << 6


def source_of(place_ref, block):
    return (((block >> 4) - place_ref[0]) & 3), ((block >> 3) & 1) == place_ref[1]


ROWS_SHAPE = (2, ONE, SLICE, ONE * BLOCK)


def early_kernel(
    place_ref, one_ref, other_ref, own_ref, low_ref, high_ref, far_factor,
    mine_out, other_out, split_high, split_low, rows, factor_ref, sem,
):
    left_half = lax.broadcasted_iota(jnp.int32, (ONE, SLICE, 128), 2) < BLOCK
    factor_copy = pltpu.make_async_copy(far_factor, factor_ref, sem)
    factor_copy.start()
    patterns = [(one_ref, 0), (one_ref, 1), (other_ref, 0), (other_ref, 1)]

    def row_step(a, carry):
        for parent, (pattern, n) in enumerate(patterns):
            block = pattern[n, a]
            step, here = source_of(place_ref, block)
            high = (block >> 2) & 1

            @pl.when(here)
            def _():
                @pl.when(step == 0)
                def _():
                    rows[parent, a] = own_ref[:, block & 7]

                @pl.when((step == 3) & (high == 0))
                def _():
                    rows[parent, a] = low_ref[:, block & 3]

                @pl.when((step == 1) & (high == 1))
                def _():
                    rows[parent, a] = high_ref[:, block & 3]

        return carry

    lax.fori_loop(0, ONE, row_step, 0)
    for parent, (pattern, n) in enumerate(patterns):
        for pair in range(ONE // 2):
            halves = []
            for side in range(2):
                source, lanes, turn = pick_lanes(pattern, n, pair, side)
                halves.append(pltpu.roll(rows[parent, :, source, :, lanes], turn, 2))
            lanes = slice(pair * 128, pair * 128 + 128)
            out = (mine_out, other_out)[parent // 2]
            out[n, :, :, lanes] = jnp.where(left_half, halves[0], halves[1])
    factor_copy.wait()
    for parent in range(2):
        split_high[parent], split_low[parent] = split(factor_ref[parent])


def early(place, pattern_one, pattern_other, factor, pieces):
    band = jax.ShapeDtypeStruct(ROWS_SHAPE, F32)
    halves = jax.ShapeDtypeStruct(factor.shape, BF16)
    return pl.pallas_call(
        early_kernel,
        out_shape=(band, band, halves, halves),
        in_specs=[SMEM] * 3 + [VMEM] * 3 + [HBM],
        out_specs=(VMEM,) * 4,
        scratch_shapes=[
            pltpu.VMEM((4, ONE, COLS, SLICE, 256), F32),
            pltpu.VMEM(factor.shape, F32),
            pltpu.SemaphoreType.DMA,
        ],
        compiler_params=pltpu.CompilerParams(vmem_limit_bytes=20 * 2**20),
        cost_estimate=pl.CostEstimate(flops=0, bytes_accessed=12 * 2**20, transcendentals=0),
        name="early",
    )(place, pattern_one, pattern_other, *pieces, *in_hbm([factor]))


def fill_kernel(whence, place_ref, *refs):
    count = (len(refs) - len(whence)) // 3
    patterns, bands, outs = refs[:count], refs[count : 2 * count], refs[-count:]
    pieces = refs[2 * count : -count]
    left_half = lax.broadcasted_iota(jnp.int32, (SLICE, 128), 1) < BLOCK
    for band, out in zip(bands, outs):
        out[...] = band[...]

    def row_step(a, carry):
        for pattern, out in zip(patterns, outs):
            for parent in range(2):
                block = pattern[parent, a]
                step, here = source_of(place_ref, block)
                high = (block >> 2) & 1

                def fill(piece):
                    for pair in range(ONE // 2):
                        halves = []
                        for side in range(2):
                            source, lanes, turn = pick_lanes(pattern, parent, pair, side)
                            halves.append(pltpu.roll(piece[source, block & 3, :, lanes], turn, 1))
                        lanes = slice(pair * 128, pair * 128 + 128)
                        out[parent, a, :, lanes] = jnp.where(left_half, halves[0], halves[1])

                @pl.when(here)
                def _():
                    for (place, half), piece in zip(whence, pieces):

                        @pl.when((step == place) & (high == half))
                        def _():
                            fill(piece)

        return carry

    lax.fori_loop(0, ONE, row_step, 0)


def fill(name, whence, place, patterns, bands, pieces):
    count = len(bands)
    return pl.pallas_call(
        functools.partial(fill_kernel, whence),
        out_shape=(jax.ShapeDtypeStruct(ROWS_SHAPE, F32),) * count,
        in_specs=[SMEM] * (1 + count) + [VMEM] * (count + len(pieces)),
        out_specs=(VMEM,) * count,
        compiler_params=pltpu.CompilerParams(vmem_limit_bytes=20 * 2**20),
        cost_estimate=pl.CostEstimate(flops=0, bytes_accessed=3 * 2**20, transcendentals=0),
        name=name,
    )(place, *patterns, *bands, *pieces)


def select_kernel(
    place_ref, one_ref, two_ref, high_ref, low_ref, mine_ref, other_ref, out_ref, band, ready, sems
):
    left_half = lax.broadcasted_iota(jnp.int32, (SLICE, 128), 1) < BLOCK

    for parent in range(2):
        for a in range(ONE):
            here = source_of(place_ref, one_ref[parent, a])[1]
            for tile in range(ONE // 2):
                lanes = slice(tile * 128, tile * 128 + 128)
                value = jnp.where(
                    here, mine_ref[parent, a, :, lanes], other_ref[parent, a, :, lanes]
                )
                at = (parent * 8 + tile) * ONE + a
                band[at] = value
                band[256 + at] = pltpu.roll(value, BLOCK, 1)

    def rows_of(parent):
        tiles = [
            band[(parent * 8 + tile) * ONE : (parent * 8 + tile + 1) * ONE].reshape(BAND, 128)
            for tile in range(ONE // 2)
        ]
        return jnp.concatenate(tiles, axis=1)

    columns = jnp.concatenate(
        [
            -product(
                split(rows_of(parent)), (high_ref[parent], low_ref[parent]), ((1,), (1,))
            )
            for parent in range(2)
        ],
        axis=1,
    )
    for child in range(COLS):
        for tile in range(3):
            ready[child, tile * BAND : tile * BAND + BAND, :] = columns[
                :, 128 * tile : 128 * tile + 128
            ]

    def send(n):
        children = slice(0, COLS) if n == 0 else slice(4 * (n - 1), 4 * n)
        part = slice(0, CHILD_TOP) if n == 0 else slice(CHILD_TOP, MESSAGE)
        return pltpu.make_async_copy(
            ready.at[children, part], out_ref.at[children, part], sems.at[n]
        )

    def child_step(child, carry):
        picks = [
            [jnp.maximum(two_ref[parent, child, n] - OWN, 0) for n in range(TWO)]
            for parent in range(2)
        ]
        places = [
            [
                256 * ((block & 1) ^ parent) + 128 * parent + ((block >> 1) << 4)
                for block in picks[parent]
            ]
            for parent in range(2)
        ]
        for unit, (k, m) in enumerate(UNITS):
            halves = [band[picks[parent][k] + places[parent][m]] for parent in range(2)]
            top = CHILD_TOP + unit * SLICE
            ready[child, top : top + SLICE, :] = jnp.where(left_half, halves[0], halves[1])
        return carry

    send(0).start()
    for n in range(4):
        lax.fori_loop(4 * n, 4 * n + 4, child_step, 0, unroll=4)
        send(n + 1).start()
    for n in range(5):
        send(n).wait()


def select(place, pattern_one, pattern_two, high, low, mine, other):
    return pl.pallas_call(
        select_kernel,
        out_shape=pltpu.HBM((COLS, MESSAGE, 128), F32),
        in_specs=[SMEM] * 3 + [VMEM] * 4,
        out_specs=HBM,
        scratch_shapes=[
            pltpu.VMEM((512, SLICE, 128), F32),
            pltpu.VMEM((COLS, MESSAGE, 128), F32),
            pltpu.SemaphoreType.DMA((5,)),
        ],
        compiler_params=pltpu.CompilerParams(vmem_limit_bytes=20 * 2**20),
        name="select",
    )(
        place,
        pattern_one,
        pattern_two,
        high,
        low,
        mine,
        pltpu.with_memory_space_constraint(other, pltpu.VMEM),
    )


def final_kernel(place_ref, two_ref, got_ref, *refs):
    (far_in, far_out, beside, chosen, near_in, near_out, sems) = (
        refs[:4], refs[4:8], refs[8:10], refs[10:12], refs[12:16], refs[16:20], refs[20],
    )
    factor_ref, _, _, child_pivot_ref = near_in
    child_factor_ref, pivot_ref = far_in[1:3]
    column_ref, diagonal_ref, child_column_ref, child_diagonal_ref = near_out
    fetches = [
        pltpu.make_async_copy(far, near, sems.at[n])
        for n, (far, near) in enumerate(zip(far_in, near_in))
    ]
    stores = [
        [
            pltpu.make_async_copy(near.at[parent], far.at[parent], sems.at[4 + 2 * n + parent])
            for parent in range(2)
        ]
        for n, (far, near) in enumerate(zip(far_out, near_out))
    ]
    fetches[0].start()
    left_half = lax.broadcasted_iota(jnp.int32, (16, 128), 1) < BLOCK
    left_block = lax.broadcasted_iota(jnp.int32, (BLOCK, 128), 1) < BLOCK
    nt = ((1,), (1,))
    for n in range(BAND):
        tiles = [got_ref[pl.ds(m * BAND + n, 16, stride=MESSAGE), :] for m in range(3)]
        here = slice(WIDTH + 16 * n, WIDTH + 16 * n + 16)
        turned = [pltpu.roll(tile, BLOCK, 1) for tile in tiles[1:]]
        beside[0][here, 0:128] = tiles[0]
        beside[0][here, 128:256] = tiles[1]
        beside[1][here, 0:128] = jnp.where(left_half, turned[0], turned[1])
        beside[1][here, 128:256] = turned[1]
    fetches[3].start()
    for parent in range(2):
        column_ref[parent] = beside[parent][WIDTH:, 0:WIDTH].T
        stores[0][parent].start()
    for unit, (k, m) in enumerate(UNITS):
        for n in range(SLICE):
            value = got_ref[pl.ds(CHILD_TOP + unit * SLICE + n, 16, stride=MESSAGE), :]
            turned = pltpu.roll(value, BLOCK, 1)
            here = slice(BLOCK * k + 16 * n, BLOCK * k + 16 * n + 16)
            lanes = slice(BLOCK * m, BLOCK * m + BLOCK)
            half = slice(0, BLOCK) if m % 2 == 0 else slice(BLOCK, 128)
            chosen[m % 2][here, lanes] = value[:, half]
            chosen[1 - m % 2][here, lanes] = turned[:, half]
    fetches[0].wait()
    diagonals = [
        pivot_ref[parent]
        - product(split(factor_ref[parent]), split(beside[parent][WIDTH:, 0:WIDTH]))
        for parent in range(2)
    ]
    for parent in range(2):
        diagonal_ref[parent] = diagonals[parent]
        beside[parent][0:WIDTH, 0:WIDTH] = diagonals[parent]
    for parent in range(2):
        stores[1][parent].start()
    row_block = lax.broadcasted_iota(jnp.int32, (WIDE, WIDE), 0) // BLOCK
    lane_block = lax.broadcasted_iota(jnp.int32, (WIDE, WIDE), 1) // BLOCK
    for parent in range(2):
        picks = [two_ref[parent, place_ref[2], n] for n in range(TWO)]
        for k in range(TWO):
            here = slice(BLOCK * k, BLOCK * k + BLOCK)
            rows = pl.ds(pl.multiple_of(picks[k] << 6, BLOCK), BLOCK)
            tiles = [beside[parent][rows, 128 * n : 128 * n + 128] for n in range(2)]
            turned = [pltpu.roll(tile, BLOCK, 1) for tile in tiles]
            even = jnp.where(
                picks[0] == 0, tiles[0], jnp.where(picks[0] == 1, turned[0], tiles[1])
            )
            odd = jnp.where(picks[1] == 1, tiles[0], turned[1])
            near = chosen[parent][here, 0:128]
            chosen[parent][here, 0:128] = jnp.where(
                left_block,
                jnp.where(picks[0] >= OWN, near, even),
                jnp.where(picks[1] >= OWN, near, odd),
            )
            if k >= 2:
                near = chosen[parent][here, 128:256]
                chosen[parent][here, 128:256] = jnp.where(
                    left_block & (picks[2] < OWN), tiles[1], near
                )
    fetches[3].wait()
    factors = [split(child_factor_ref[parent, 0]) for parent in range(2)]
    results = []
    for parent in range(2):
        lower = chosen[parent][...]
        whole = jnp.where(row_block >= lane_block, lower, lower.T)
        results.append(-product(factors[parent], split(whole)))
    for parent in range(2):
        child_column_ref[parent, 0] = results[parent]
    for parent in range(2):
        stores[2][parent].start()
    diagonals = [
        child_pivot_ref[parent, 0] - product(factors[parent], split(results[parent]), nt)
        for parent in range(2)
    ]
    for parent in range(2):
        child_diagonal_ref[parent, 0] = diagonals[parent]
    for parent in range(2):
        stores[3][parent].start()
    for pair in stores:
        for store in pair:
            store.wait()


def finish(place, pattern_two, got, arrays):
    shapes = (
        (2, WIDTH, ONE * BLOCK),
        (2, WIDTH, WIDTH),
        (2, 1, WIDTH, WIDE),
        (2, 1, WIDTH, WIDTH),
    )
    return pl.pallas_call(
        final_kernel,
        out_shape=tuple(pltpu.HBM(shape, F32) for shape in shapes),
        in_specs=[SMEM, SMEM, VMEM] + [HBM, VMEM, VMEM, HBM],
        out_specs=(HBM,) * 4,
        scratch_shapes=[pltpu.VMEM((WIDTH + ONE * BLOCK, 256), F32)] * 2
        + [pltpu.VMEM((WIDE, WIDE), F32)] * 2
        + [pltpu.VMEM(array.shape, array.dtype) for array in arrays]
        + [pltpu.VMEM(shape, F32) for shape in shapes]
        + [pltpu.SemaphoreType.DMA((12,))],
        compiler_params=pltpu.CompilerParams(vmem_limit_bytes=24 * 2**20),
        name="finish",
    )(place, pattern_two, got, *in_hbm(arrays[:1]), *arrays[1:3], *in_hbm(arrays[3:]))


FORWARD = [(r, (r + 2) % ROWS) for r in range(ROWS)]
BACKWARD = [(r, (r - 2) % ROWS) for r in range(ROWS)]
SWAP = [(r, r ^ 1) for r in range(ROWS)]


def per_device(
    root_inverse, factor_one, pivot_one, pattern_one, factor_two, pivot_two, pattern_two
):
    row = lax.axis_index("row")
    col = lax.axis_index("col")
    place = jnp.stack([row >> 1, row & 1, col]).astype(jnp.int32)
    factor_one = jnp.swapaxes(factor_one, 1, 2)
    factor_two = jnp.swapaxes(factor_two, 2, 3)
    shard = lax.all_to_all(pack(root_inverse), "col", 0, 0, tiled=True)
    shard, pattern = lax.optimization_barrier((shard, pattern_one))
    pattern_other = lax.ppermute(pattern, "row", SWAP)
    halves = [shard[:, :4], shard[:, 4:]]
    behind = [lax.ppermute(half, "row", FORWARD) for half in halves]
    ahead = [lax.ppermute(half, "row", BACKWARD) for half in halves]
    across = [lax.ppermute(behind[0], "row", FORWARD), lax.ppermute(ahead[1], "row", BACKWARD)]
    mine, other, high, low = early(
        place, pattern_one, pattern_other, factor_one, [shard, behind[0], ahead[1]]
    )
    mine, other = fill(
        "second",
        ((1, 0), (3, 1)),
        place,
        (pattern_one, pattern_other),
        (mine, other),
        (ahead[0], behind[1]),
    )
    relayed = ((2, 0), (2, 1))
    (other,) = fill("last", relayed, place, (pattern_other,), (other,), across)
    other = lax.ppermute(other, "row", SWAP)
    (mine,) = fill("last", relayed, place, (pattern_one,), (mine,), across)
    message = select(place, pattern_one, pattern_two, high, low, mine, other)
    got = lax.all_to_all(message, "col", 0, 0, tiled=True)
    column_one, diagonal_one, column_two, diagonal_two = finish(
        place,
        pattern_two,
        got.reshape(COLS * MESSAGE, 128),
        (factor_one, factor_two, pivot_one, pivot_two),
    )
    return (
        jnp.swapaxes(column_one, 1, 2),
        diagonal_one,
        jnp.swapaxes(column_two, 2, 3),
        diagonal_two,
    )


def solution(mesh):
    placed = (
        P("row", "col"),
        P("row", None, None),
        P("row", None, None),
        P("row", None),
        P("row", "col", None, None),
        P("row", "col", None, None),
        P("row", None, None),
    )
    return jax.shard_map(
        per_device,
        mesh=mesh,
        in_specs=placed,
        out_specs=(
            P("row", None, None),
            P("row", None, None),
            P("row", "col", None, None),
            P("row", "col", None, None),
        ),
        check_vma=False,
    )
```

```python
import functools

import jax
import jax.numpy as jnp
from jax import lax
from jax.experimental import pallas as pl
from jax.experimental.pallas import tpu as pltpu
from jax.sharding import PartitionSpec as P

F32 = jnp.float32
BF16 = jnp.bfloat16
BLOCK = 64
WIDTH = 192
ONE = 16
TWO = 6
OWN = 3
COLS = 16
ROWS = 8
SLICE = 4
UNITS = [(k, m) for k in range(TWO) for m in range(k + 1)]
BAND = ONE * SLICE
CHILD_TOP = 3 * BAND
MESSAGE = 280
WIDE = TWO * BLOCK
VMEM = pl.BlockSpec(memory_space=pltpu.VMEM)
SMEM = pl.BlockSpec(memory_space=pltpu.SMEM)
ANY = pl.BlockSpec(memory_space=pl.ANY)
HBM = pl.BlockSpec(memory_space=pltpu.HBM)


def in_hbm(arrays):
    return [pltpu.with_memory_space_constraint(array, pltpu.HBM) for array in arrays]


def split(value):
    high = value.astype(BF16)
    low = (value - high.astype(F32)).astype(BF16)
    return high, low


def product(left, right, dims=((1,), (0,))):
    def one(a, b):
        return lax.dot_general(a, b, (dims, ((), ())), preferred_element_type=F32)

    (lh, ll), (rh, rl) = left, right
    return one(lh, rh) + (one(lh, rl) + one(ll, rh))


def pack_kernel(root_ref, out_ref, near, ready, sems):
    def fetch(n, tile):
        here, lanes = slice(BLOCK * n, BLOCK * n + BLOCK), slice(128 * tile, 128 * tile + 128)
        return pltpu.make_async_copy(
            root_ref.at[here, lanes], near.at[tile, here], sems.at[0, n, tile]
        )

    def store(n):
        return pltpu.make_async_copy(ready.at[n], out_ref.at[:, n], sems.at[1, n, 0])

    for n in range(8):
        for tile in range(2):
            fetch(n, tile).start()
    for n in range(8):
        for tile in range(2):
            fetch(n, tile).wait()
            for place in range(COLS):
                ready[n, place, :, 128 * tile : 128 * tile + 128] = near[
                    tile, pl.ds(BLOCK * n + place, SLICE, stride=16), :
                ]
        store(n).start()
    for n in range(8):
        store(n).wait()


def pack(root):
    return pl.pallas_call(
        pack_kernel,
        out_shape=pltpu.HBM((COLS, 8, SLICE, 256), F32),
        in_specs=[HBM],
        out_specs=HBM,
        scratch_shapes=[
            pltpu.VMEM((2, 512, 128), F32),
            pltpu.VMEM((8, COLS, SLICE, 256), F32),
            pltpu.SemaphoreType.DMA((2, 8, 2)),
        ],
        name="pack",
    )(*in_hbm([root]))


def pick_lanes(one_ref, parent, pair, side):
    block = one_ref[parent, 2 * pair + side]
    lanes = pl.ds(pl.multiple_of(((block >> 1) & 1) << 7, 128), 128)
    return block >> 2, lanes, ((block & 1) ^ side) << 6


def source_of(place_ref, block):
    return (((block >> 4) - place_ref[0]) & 3), ((block >> 3) & 1) == place_ref[1]


ROWS_SHAPE = (2, ONE, SLICE, ONE * BLOCK)


def early_kernel(
    place_ref, one_ref, other_ref, own_ref, low_ref, high_ref, far_factor,
    mine_out, other_out, split_high, split_low, rows, factor_ref, sem,
):
    left_half = lax.broadcasted_iota(jnp.int32, (ONE, SLICE, 128), 2) < BLOCK
    factor_copy = pltpu.make_async_copy(far_factor, factor_ref, sem)
    factor_copy.start()
    patterns = [(one_ref, 0), (one_ref, 1), (other_ref, 0), (other_ref, 1)]

    def row_step(a, carry):
        for parent, (pattern, n) in enumerate(patterns):
            block = pattern[n, a]
            step, here = source_of(place_ref, block)
            high = (block >> 2) & 1

            @pl.when(here)
            def _():
                @pl.when(step == 0)
                def _():
                    rows[parent, a] = own_ref[:, block & 7]

                @pl.when((step == 3) & (high == 0))
                def _():
                    rows[parent, a] = low_ref[:, block & 3]

                @pl.when((step == 1) & (high == 1))
                def _():
                    rows[parent, a] = high_ref[:, block & 3]

        return carry

    lax.fori_loop(0, ONE, row_step, 0)
    for parent, (pattern, n) in enumerate(patterns):
        for pair in range(ONE // 2):
            halves = []
            for side in range(2):
                source, lanes, turn = pick_lanes(pattern, n, pair, side)
                halves.append(pltpu.roll(rows[parent, :, source, :, lanes], turn, 2))
            lanes = slice(pair * 128, pair * 128 + 128)
            out = (mine_out, other_out)[parent // 2]
            out[n, :, :, lanes] = jnp.where(left_half, halves[0], halves[1])
    factor_copy.wait()
    for parent in range(2):
        split_high[parent], split_low[parent] = split(factor_ref[parent])


def early(place, pattern_one, pattern_other, factor, pieces):
    band = jax.ShapeDtypeStruct(ROWS_SHAPE, F32)
    halves = jax.ShapeDtypeStruct(factor.shape, BF16)
    return pl.pallas_call(
        early_kernel,
        out_shape=(band, band, halves, halves),
        in_specs=[SMEM] * 3 + [VMEM] * 3 + [HBM],
        out_specs=(VMEM,) * 4,
        scratch_shapes=[
            pltpu.VMEM((4, ONE, COLS, SLICE, 256), F32),
            pltpu.VMEM(factor.shape, F32),
            pltpu.SemaphoreType.DMA,
        ],
        compiler_params=pltpu.CompilerParams(vmem_limit_bytes=20 * 2**20),
        cost_estimate=pl.CostEstimate(flops=0, bytes_accessed=12 * 2**20, transcendentals=0),
        name="early",
    )(place, pattern_one, pattern_other, *pieces, *in_hbm([factor]))


def fill_kernel(whence, place_ref, *refs):
    count = (len(refs) - len(whence)) // 3
    patterns, bands, outs = refs[:count], refs[count : 2 * count], refs[-count:]
    pieces = refs[2 * count : -count]
    left_half = lax.broadcasted_iota(jnp.int32, (SLICE, 128), 1) < BLOCK
    for band, out in zip(bands, outs):
        out[...] = band[...]

    def row_step(a, carry):
        for pattern, out in zip(patterns, outs):
            for parent in range(2):
                block = pattern[parent, a]
                step, here = source_of(place_ref, block)
                high = (block >> 2) & 1

                def fill(piece):
                    for pair in range(ONE // 2):
                        halves = []
                        for side in range(2):
                            source, lanes, turn = pick_lanes(pattern, parent, pair, side)
                            halves.append(pltpu.roll(piece[source, block & 3, :, lanes], turn, 1))
                        lanes = slice(pair * 128, pair * 128 + 128)
                        out[parent, a, :, lanes] = jnp.where(left_half, halves[0], halves[1])

                @pl.when(here)
                def _():
                    for at in range(0, len(whence), 2):
                        if whence[at][0] == whence[at + 1][0]:

                            @pl.when(step == whence[at][0])
                            def _():
                                for n in (at, at + 1):

                                    @pl.when(high == whence[n][1])
                                    def _():
                                        fill(pieces[n])

                        else:
                            for n in (at, at + 1):

                                @pl.when((step == whence[n][0]) & (high == whence[n][1]))
                                def _():
                                    fill(pieces[n])

        return carry

    lax.fori_loop(0, ONE, row_step, 0)


def fill(name, whence, place, patterns, bands, pieces):
    count = len(bands)
    return pl.pallas_call(
        functools.partial(fill_kernel, whence),
        out_shape=(jax.ShapeDtypeStruct(ROWS_SHAPE, F32),) * count,
        in_specs=[SMEM] * (1 + count) + [VMEM] * (count + len(pieces)),
        out_specs=(VMEM,) * count,
        compiler_params=pltpu.CompilerParams(vmem_limit_bytes=20 * 2**20),
        cost_estimate=pl.CostEstimate(flops=0, bytes_accessed=3 * 2**20, transcendentals=0),
        name=name,
    )(place, *patterns, *bands, *pieces)


def select_kernel(
    place_ref, one_ref, two_ref, high_ref, low_ref, mine_ref, other_ref, out_ref, band, ready, sems
):
    left_half = lax.broadcasted_iota(jnp.int32, (SLICE, 128), 1) < BLOCK

    for parent in range(2):
        for a in range(ONE):
            here = source_of(place_ref, one_ref[parent, a])[1]
            for tile in range(ONE // 2):
                lanes = slice(tile * 128, tile * 128 + 128)
                value = jnp.where(
                    here, mine_ref[parent, a, :, lanes], other_ref[parent, a, :, lanes]
                )
                at = (parent * 8 + tile) * ONE + a
                band[at] = value
                band[256 + at] = pltpu.roll(value, BLOCK, 1)

    def rows_of(parent):
        tiles = [
            band[(parent * 8 + tile) * ONE : (parent * 8 + tile + 1) * ONE].reshape(BAND, 128)
            for tile in range(ONE // 2)
        ]
        return jnp.concatenate(tiles, axis=1)

    columns = jnp.concatenate(
        [
            -product(
                split(rows_of(parent)), (high_ref[parent], low_ref[parent]), ((1,), (1,))
            )
            for parent in range(2)
        ],
        axis=1,
    )
    for child in range(COLS):
        for tile in range(3):
            ready[child, tile * BAND : tile * BAND + BAND, :] = columns[
                :, 128 * tile : 128 * tile + 128
            ]

    def send(n):
        children = slice(0, COLS) if n == 0 else slice(4 * (n - 1), 4 * n)
        part = slice(0, CHILD_TOP) if n == 0 else slice(CHILD_TOP, MESSAGE)
        return pltpu.make_async_copy(
            ready.at[children, part], out_ref.at[children, part], sems.at[n]
        )

    def child_step(child, carry):
        picks = [
            [jnp.maximum(two_ref[parent, child, n] - OWN, 0) for n in range(TWO)]
            for parent in range(2)
        ]
        places = [
            [
                256 * ((block & 1) ^ parent) + 128 * parent + ((block >> 1) << 4)
                for block in picks[parent]
            ]
            for parent in range(2)
        ]
        for unit, (k, m) in enumerate(UNITS):
            halves = [band[picks[parent][k] + places[parent][m]] for parent in range(2)]
            top = CHILD_TOP + unit * SLICE
            ready[child, top : top + SLICE, :] = jnp.where(left_half, halves[0], halves[1])
        return carry

    send(0).start()
    for n in range(4):
        lax.fori_loop(4 * n, 4 * n + 4, child_step, 0, unroll=4)
        send(n + 1).start()
    for n in range(5):
        send(n).wait()


def select(place, pattern_one, pattern_two, high, low, mine, other):
    return pl.pallas_call(
        select_kernel,
        out_shape=pltpu.HBM((COLS, MESSAGE, 128), F32),
        in_specs=[SMEM] * 3 + [VMEM] * 4,
        out_specs=HBM,
        scratch_shapes=[
            pltpu.VMEM((512, SLICE, 128), F32),
            pltpu.VMEM((COLS, MESSAGE, 128), F32),
            pltpu.SemaphoreType.DMA((5,)),
        ],
        compiler_params=pltpu.CompilerParams(vmem_limit_bytes=20 * 2**20),
        name="select",
    )(
        place,
        pattern_one,
        pattern_two,
        high,
        low,
        mine,
        pltpu.with_memory_space_constraint(other, pltpu.VMEM),
    )


def final_kernel(place_ref, two_ref, got_ref, *refs):
    (far_in, far_out, beside, chosen, near_in, near_out, sems) = (
        refs[:4], refs[4:8], refs[8:10], refs[10:12], refs[12:16], refs[16:20], refs[20],
    )
    factor_ref, _, _, child_pivot_ref = near_in
    child_factor_ref, pivot_ref = far_in[1:3]
    column_ref, diagonal_ref, child_column_ref, child_diagonal_ref = near_out
    fetches = [
        pltpu.make_async_copy(far, near, sems.at[n])
        for n, (far, near) in enumerate(zip(far_in, near_in))
    ]
    stores = [
        [
            pltpu.make_async_copy(near.at[parent], far.at[parent], sems.at[4 + 2 * n + parent])
            for parent in range(2)
        ]
        for n, (far, near) in enumerate(zip(far_out, near_out))
    ]
    fetches[0].start()
    left_half = lax.broadcasted_iota(jnp.int32, (16, 128), 1) < BLOCK
    left_block = lax.broadcasted_iota(jnp.int32, (BLOCK, 128), 1) < BLOCK
    nt = ((1,), (1,))
    for n in range(BAND):
        tiles = [got_ref[pl.ds(m * BAND + n, 16, stride=MESSAGE), :] for m in range(3)]
        here = slice(WIDTH + 16 * n, WIDTH + 16 * n + 16)
        turned = [pltpu.roll(tile, BLOCK, 1) for tile in tiles[1:]]
        beside[0][here, 0:128] = tiles[0]
        beside[0][here, 128:256] = tiles[1]
        beside[1][here, 0:128] = jnp.where(left_half, turned[0], turned[1])
        beside[1][here, 128:256] = turned[1]
    fetches[3].start()
    for parent in range(2):
        column_ref[parent] = beside[parent][WIDTH:, 0:WIDTH].T
        stores[0][parent].start()
    for unit, (k, m) in enumerate(UNITS):
        for n in range(SLICE):
            value = got_ref[pl.ds(CHILD_TOP + unit * SLICE + n, 16, stride=MESSAGE), :]
            turned = pltpu.roll(value, BLOCK, 1)
            here = slice(BLOCK * k + 16 * n, BLOCK * k + 16 * n + 16)
            lanes = slice(BLOCK * m, BLOCK * m + BLOCK)
            half = slice(0, BLOCK) if m % 2 == 0 else slice(BLOCK, 128)
            chosen[m % 2][here, lanes] = value[:, half]
            chosen[1 - m % 2][here, lanes] = turned[:, half]
    fetches[0].wait()
    diagonals = [
        pivot_ref[parent]
        - product(split(factor_ref[parent]), split(beside[parent][WIDTH:, 0:WIDTH]))
        for parent in range(2)
    ]
    for parent in range(2):
        diagonal_ref[parent] = diagonals[parent]
        beside[parent][0:WIDTH, 0:WIDTH] = diagonals[parent]
    for parent in range(2):
        stores[1][parent].start()
    row_block = lax.broadcasted_iota(jnp.int32, (WIDE, WIDE), 0) // BLOCK
    lane_block = lax.broadcasted_iota(jnp.int32, (WIDE, WIDE), 1) // BLOCK
    for parent in range(2):
        picks = [two_ref[parent, place_ref[2], n] for n in range(TWO)]
        for k in range(TWO):
            here = slice(BLOCK * k, BLOCK * k + BLOCK)
            rows = pl.ds(pl.multiple_of(picks[k] << 6, BLOCK), BLOCK)
            tiles = [beside[parent][rows, 128 * n : 128 * n + 128] for n in range(2)]
            turned = [pltpu.roll(tile, BLOCK, 1) for tile in tiles]
            even = jnp.where(
                picks[0] == 0, tiles[0], jnp.where(picks[0] == 1, turned[0], tiles[1])
            )
            odd = jnp.where(picks[1] == 1, tiles[0], turned[1])
            near = chosen[parent][here, 0:128]
            chosen[parent][here, 0:128] = jnp.where(
                left_block,
                jnp.where(picks[0] >= OWN, near, even),
                jnp.where(picks[1] >= OWN, near, odd),
            )
            if k >= 2:
                near = chosen[parent][here, 128:256]
                chosen[parent][here, 128:256] = jnp.where(
                    left_block & (picks[2] < OWN), tiles[1], near
                )
    fetches[3].wait()
    factors = [split(child_factor_ref[parent, 0]) for parent in range(2)]
    results = []
    for parent in range(2):
        lower = chosen[parent][...]
        whole = jnp.where(row_block >= lane_block, lower, lower.T)
        results.append(-product(factors[parent], split(whole)))
    for parent in range(2):
        child_column_ref[parent, 0] = results[parent]
    for parent in range(2):
        stores[2][parent].start()
    diagonals = [
        child_pivot_ref[parent, 0] - product(factors[parent], split(results[parent]), nt)
        for parent in range(2)
    ]
    for parent in range(2):
        child_diagonal_ref[parent, 0] = diagonals[parent]
    for parent in range(2):
        stores[3][parent].start()
    for pair in stores:
        for store in pair:
            store.wait()


def finish(place, pattern_two, got, arrays):
    shapes = (
        (2, WIDTH, ONE * BLOCK),
        (2, WIDTH, WIDTH),
        (2, 1, WIDTH, WIDE),
        (2, 1, WIDTH, WIDTH),
    )
    return pl.pallas_call(
        final_kernel,
        out_shape=tuple(pltpu.HBM(shape, F32) for shape in shapes),
        in_specs=[SMEM, SMEM, VMEM] + [HBM, VMEM, VMEM, HBM],
        out_specs=(HBM,) * 4,
        scratch_shapes=[pltpu.VMEM((WIDTH + ONE * BLOCK, 256), F32)] * 2
        + [pltpu.VMEM((WIDE, WIDE), F32)] * 2
        + [pltpu.VMEM(array.shape, array.dtype) for array in arrays]
        + [pltpu.VMEM(shape, F32) for shape in shapes]
        + [pltpu.SemaphoreType.DMA((12,))],
        compiler_params=pltpu.CompilerParams(vmem_limit_bytes=24 * 2**20),
        name="finish",
    )(place, pattern_two, got, *in_hbm(arrays[:1]), *arrays[1:3], *in_hbm(arrays[3:]))


FORWARD = [(r, (r + 2) % ROWS) for r in range(ROWS)]
BACKWARD = [(r, (r - 2) % ROWS) for r in range(ROWS)]
SWAP = [(r, r ^ 1) for r in range(ROWS)]


def per_device(
    root_inverse, factor_one, pivot_one, pattern_one, factor_two, pivot_two, pattern_two
):
    row = lax.axis_index("row")
    col = lax.axis_index("col")
    place = jnp.stack([row >> 1, row & 1, col]).astype(jnp.int32)
    factor_one = jnp.swapaxes(factor_one, 1, 2)
    factor_two = jnp.swapaxes(factor_two, 2, 3)
    shard = lax.all_to_all(pack(root_inverse), "col", 0, 0, tiled=True)
    shard, pattern = lax.optimization_barrier((shard, pattern_one))
    pattern_other = lax.ppermute(pattern, "row", SWAP)
    halves = [shard[:, :4], shard[:, 4:]]
    behind = [lax.ppermute(half, "row", FORWARD) for half in halves]
    ahead = [lax.ppermute(half, "row", BACKWARD) for half in halves]
    across = [lax.ppermute(behind[0], "row", FORWARD), lax.ppermute(ahead[1], "row", BACKWARD)]
    mine, other, high, low = early(
        place, pattern_one, pattern_other, factor_one, [shard, behind[0], ahead[1]]
    )
    mine, other = fill(
        "second",
        ((1, 0), (3, 1)),
        place,
        (pattern_one, pattern_other),
        (mine, other),
        (ahead[0], behind[1]),
    )
    relayed = ((2, 0), (2, 1))
    (other,) = fill("last", relayed, place, (pattern_other,), (other,), across)
    other = lax.ppermute(other, "row", SWAP)
    (mine,) = fill("last", relayed, place, (pattern_one,), (mine,), across)
    message = select(place, pattern_one, pattern_two, high, low, mine, other)
    got = lax.all_to_all(message, "col", 0, 0, tiled=True)
    column_one, diagonal_one, column_two, diagonal_two = finish(
        place,
        pattern_two,
        got.reshape(COLS * MESSAGE, 128),
        (factor_one, factor_two, pivot_one, pivot_two),
    )
    return (
        jnp.swapaxes(column_one, 1, 2),
        diagonal_one,
        jnp.swapaxes(column_two, 2, 3),
        diagonal_two,
    )


def solution(mesh):
    placed = (
        P("row", "col"),
        P("row", None, None),
        P("row", None, None),
        P("row", None),
        P("row", "col", None, None),
        P("row", "col", None, None),
        P("row", None, None),
    )
    return jax.shard_map(
        per_device,
        mesh=mesh,
        in_specs=placed,
        out_specs=(
            P("row", None, None),
            P("row", None, None),
            P("row", "col", None, None),
            P("row", "col", None, None),
        ),
        check_vma=False,
    )
```
